512 devices in a mesh: tm: 64 (over z, y), space: 8 (over x, core).
Axes of the slice: x: 4, y: 8, z: 8, core: 2. Of those that a mesh axis runs over, the one named last changes fastest.
Arguments:
- frames: bfloat16 [128, 32, 64, 256], P('tm', 'space'), may hold values from -54 to 54
- cotangent: bfloat16 [128, 32, 64, 256], P('tm', 'space'), may hold values from -6 to 6
- w_spatial: bfloat16 [3, 3, 256, 256], replicated, may hold values from -0.125 to 0.125
- w_temporal: bfloat16 [3, 256, 256], replicated, may hold values from -0.21875 to 0.21875
- norm_gain: float32 [256], replicated, may hold values from 0.1 to 1.9
- w_query: bfloat16 [256, 256], replicated, may hold values from -0.375 to 0.375
- w_key: bfloat16 [256, 256], replicated, may hold values from -0.375 to 0.375
- w_value: bfloat16 [256, 256], replicated, may hold values from -0.375 to 0.375
- w_out: bfloat16 [256, 256], replicated, may hold values from -0.375 to 0.375
Outputs:
- input_grad: bfloat16 [128, 32, 64, 256], P('tm', 'space')
The draws below stay inside these ranges and needn't reach their ends.
All inputs are finite; a program needn't handle non-finite values.
Results may differ from the reference program's by a relative error of at most 0.017.
Values may be sent and summed in bfloat16 or wider, within the bound.
A program may use at most 64 MiB of HBM per device.

```python
import math
import jax
import jax.numpy as jnp
from jax import lax

C = 256
COLS = 64
FRAMES = 128
ROWS = 32


def draw_frames(key, part):
    noise_key, channel_key, token_key = jax.random.split(key, 3)
    full_shape = (FRAMES, ROWS, COLS, C)
    noise_field = jnp.clip(jax.random.normal(noise_key, full_shape, jnp.float32), -6.0, 6.0)
    lowest = 0.3
    highest = 3.0
    channel_scale = jnp.exp(jax.random.uniform(channel_key, (C,), jnp.float32, math.log(lowest), math.log(highest)))
    token_scale = jnp.exp(jax.random.uniform(token_key, (FRAMES, ROWS, COLS, 1), jnp.float32, math.log(lowest), math.log(highest)))
    return (noise_field * channel_scale * token_scale).astype(jnp.bfloat16)


def steps_of(rng, shape, cuts, least, largest):
    def one(dim, parts):
        steps = jax.random.uniform(jax.random.fold_in(jax.random.fold_in(rng, 6), dim), (parts,), jnp.float32, least / len(cuts), largest / len(cuts))
        return jnp.repeat(jnp.exp(steps), shape[dim] // parts).reshape((-1,) + (1,) * (len(shape) - dim - 1))

    loudness = one(*cuts[0])
    for cut in cuts[1:]:
        loudness = loudness * one(*cut)
    return loudness


def centred(stream_key, extent, scale, reach, cuts=(), kind=jnp.bfloat16):
    loudness = steps_of(stream_key, extent, cuts, -0.22, 0.18) if cuts else 1.0
    array = jax.random.normal(stream_key, extent, jnp.float32) * scale * loudness
    return jnp.minimum(jnp.maximum(array, -reach), reach).astype(kind)


def setup_inputs(seed: int = 0) -> dict:
    key_of = jax.random.split(jax.random.key(seed), 10)
    frames = draw_frames(jax.random.fold_in(key_of[9], 71), 0)
    cotangent = centred(key_of[1], (FRAMES, ROWS, COLS, C), 1.0, 6.0, ((0, 64), (1, 8)))
    w_spatial = centred(key_of[2], (3, 3, C, C), (9 * C) ** -0.5, 0.125)
    w_temporal = centred(key_of[3], (3, C, C), (3 * C) ** -0.5, 0.21875)
    norm_gain = jnp.clip(1.0 + 0.18 * jax.random.normal(key_of[4], (C,), jnp.float32), 0.1, 1.9)
    w_query = centred(key_of[5], (C, C), C ** -0.5, 0.375)
    w_key = centred(key_of[6], (C, C), C ** -0.5, 0.375)
    w_value = centred(key_of[7], (C, C), C ** -0.5, 0.375)
    w_out = centred(key_of[8], (C, C), C ** -0.5, 0.375)
    return dict(frames=frames, cotangent=cotangent, w_spatial=w_spatial, w_temporal=w_temporal, norm_gain=norm_gain, w_query=w_query, w_key=w_key, w_value=w_value, w_out=w_out)


EPSILON = 1e-05

def spatial_frame(one_frame, w_spatial):
    padded = jnp.pad(one_frame, ((1, 1), (1, 1), (0, 0)))
    running = jnp.zeros((ROWS * COLS, C), jnp.float32)
    for tap_row in range(3):
        for tap_col in range(3):
            window = padded[tap_row:tap_row + ROWS, tap_col:tap_col + COLS].reshape(ROWS * COLS, C)
            running = running + jnp.dot(window, w_spatial[tap_row, tap_col], preferred_element_type=jnp.float32)
    return running.astype(jnp.bfloat16).reshape(ROWS, COLS, C)

def norm_forward(hidden, norm_gain):
    hidden_wide = hidden.astype(jnp.float32)
    inverse = lax.rsqrt(lax.optimization_barrier(jnp.mean(hidden_wide * hidden_wide, axis=-1, keepdims=True)) + EPSILON)
    normed = (hidden_wide * inverse * norm_gain).astype(jnp.bfloat16)
    return (hidden_wide, inverse, normed)

def norm_backward(hidden_wide, inverse, norm_gain, normed_grad):
    scaled = normed_grad * norm_gain
    cubed = inverse * inverse * inverse
    result = inverse * scaled - hidden_wide * cubed * lax.optimization_barrier(jnp.mean(hidden_wide * scaled, axis=-1, keepdims=True))
    return result.astype(jnp.bfloat16)

def attention_grads(query_rows, key_rows, value_rows, out_grad):
    frame_total = query_rows.shape[0]
    score_scale = 1.0 / math.sqrt(C)
    position = jnp.arange(frame_total)
    causal_mask = position[None, :] <= position[:, None]
    query_wide = query_rows.astype(jnp.float32)
    key_wide = key_rows.astype(jnp.float32)
    scores = jnp.einsum('fpc,gpc->pfg', query_wide, key_wide) * score_scale
    weights = jnp.where(causal_mask[None], jnp.exp(scores), 0.0)
    attn_probs = weights / lax.optimization_barrier(jnp.sum(weights, axis=-1, keepdims=True))
    probs_low = attn_probs.astype(jnp.bfloat16)
    grad_wide = out_grad.astype(jnp.float32)
    prob_grad = jnp.einsum('fpc,gpc->pfg', grad_wide, value_rows.astype(jnp.float32))
    value_grad = jnp.einsum('pfg,fpc->gpc', probs_low.astype(jnp.float32), grad_wide).astype(jnp.bfloat16)
    centre = lax.optimization_barrier(jnp.sum(attn_probs * prob_grad, axis=-1, keepdims=True))
    score_grad = (attn_probs * (prob_grad - centre) * score_scale).astype(jnp.bfloat16)
    score_wide = score_grad.astype(jnp.float32)
    query_grad = jnp.einsum('pfg,gpc->fpc', score_wide, key_wide).astype(jnp.bfloat16)
    key_grad = jnp.einsum('pfg,fpc->gpc', score_wide, query_wide).astype(jnp.bfloat16)
    return (query_grad, key_grad, value_grad)

def attend_block(hidden_rows, grad_rows, norm_gain, w_query, w_key, w_value, w_out):
    hidden_wide, inverse, normed = norm_forward(hidden_rows, norm_gain)
    query_rows = jnp.dot(normed, w_query, preferred_element_type=jnp.float32).astype(jnp.bfloat16)
    key_rows = jnp.dot(normed, w_key, preferred_element_type=jnp.float32).astype(jnp.bfloat16)
    value_rows = jnp.dot(normed, w_value, preferred_element_type=jnp.float32).astype(jnp.bfloat16)
    out_grad = jnp.dot(grad_rows, w_out.T, preferred_element_type=jnp.float32).astype(jnp.bfloat16)
    query_grad, key_grad, value_grad = attention_grads(query_rows, key_rows, value_rows, out_grad)
    normed_grad = jnp.dot(query_grad, w_query.T, preferred_element_type=jnp.float32)
    normed_grad = normed_grad + jnp.dot(key_grad, w_key.T, preferred_element_type=jnp.float32)
    normed_grad = normed_grad + jnp.dot(value_grad, w_value.T, preferred_element_type=jnp.float32)
    return norm_backward(hidden_wide, inverse, norm_gain, normed_grad)

def reference(frames, cotangent, w_spatial, w_temporal, norm_gain, w_query, w_key, w_value, w_out):
    spatial = lax.map(lambda one_frame: spatial_frame(one_frame, w_spatial), frames)
    zeros_two = jnp.zeros((2, ROWS, COLS, C), spatial.dtype)
    padded_past = jnp.concatenate([zeros_two, spatial], 0)
    flat_temporal = w_temporal.reshape(3 * C, C)

    def temporal_frame(frame_items):
        current, one_back, two_back, one_frame = frame_items
        stacked = jnp.concatenate([current, one_back, two_back], -1).reshape(ROWS * COLS, 3 * C)
        mixed_sum = jnp.dot(stacked, flat_temporal, preferred_element_type=jnp.float32).reshape(ROWS, COLS, C)
        return (one_frame.astype(jnp.float32) + mixed_sum).astype(jnp.bfloat16)
    hidden = lax.map(temporal_frame, (padded_past[2:], padded_past[1:-1], padded_past[:-2], frames))

    def attend_row(frame_items):
        hidden_rows, grad_rows = frame_items
        return attend_block(hidden_rows, grad_rows, norm_gain, w_query, w_key, w_value, w_out)
    attn_grad = lax.map(attend_row, (jnp.swapaxes(hidden, 0, 1), jnp.swapaxes(cotangent, 0, 1)))
    attn_grad = jnp.swapaxes(attn_grad, 0, 1)
    total_grad = (cotangent.astype(jnp.float32) + attn_grad.astype(jnp.float32)).astype(jnp.bfloat16)
    ahead_frames = jnp.concatenate([total_grad, zeros_two.astype(total_grad.dtype)], 0)
    flat_back = jnp.transpose(w_temporal, (0, 2, 1)).reshape(3 * C, C)

    def temporal_back(frame_items):
        current, one_ahead, two_ahead = frame_items
        stacked = jnp.concatenate([current, one_ahead, two_ahead], -1).reshape(ROWS * COLS, 3 * C)
        mixed_sum = jnp.dot(stacked, flat_back, preferred_element_type=jnp.float32)
        return mixed_sum.astype(jnp.bfloat16).reshape(ROWS, COLS, C)
    spatial_grad = lax.map(temporal_back, (ahead_frames[:-2], ahead_frames[1:-1], ahead_frames[2:]))

    def input_frame(frame_items):
        grad_frame, total_frame = frame_items
        padded = jnp.pad(grad_frame, ((1, 1), (1, 1), (0, 0)))
        running = total_frame.astype(jnp.float32).reshape(ROWS * COLS, C)
        for tap_row in range(3):
            for tap_col in range(3):
                window = padded[2 - tap_row:2 - tap_row + ROWS, 2 - tap_col:2 - tap_col + COLS].reshape(ROWS * COLS, C)
                running = running + jnp.dot(window, w_spatial[tap_row, tap_col].T, preferred_element_type=jnp.float32)
        return running.astype(jnp.bfloat16).reshape(ROWS, COLS, C)
    return lax.map(input_frame, (spatial_grad, total_grad))
```

```python
import jax
import jax.numpy as jnp
from jax import lax
from jax.experimental import pallas as pl
from jax.experimental.pallas import tpu as pltpu
from jax.sharding import PartitionSpec as P

EPSILON = 1e-05
MESH = pl.DeviceIdType.MESH
BF = jnp.bfloat16
F32 = jnp.float32
T = 512
C = 256


def mm(a, b):
    return jnp.dot(a, b, preferred_element_type=F32)


def mm_nt(a, b):
    return lax.dot_general(a, b, (((1,), (1,)), ((), ())), preferred_element_type=F32)


def mm_tn(a, b):
    return lax.dot_general(a, b, (((0,), (0,)), ((), ())), preferred_element_type=F32)


def iota(shape, dim):
    return lax.broadcasted_iota(jnp.int32, shape, dim)


def to_tiles(x):
    x = x.reshape(64, 8, C)
    return jnp.concatenate([x[:, :, :128], x[:, :, 128:]], axis=1).astype(BF)


def from_tiles(x):
    x = x.astype(F32)
    return jnp.concatenate([x[:, :8], x[:, 8:]], axis=2).reshape(T, C)


def roll_rows(x, distance):
    return pltpu.roll(x, distance % x.shape[0], 0)


def kernel(
    frames_h, cot_h, ws_h, wt_h, gain_h, wq_h, wk_h, wv_h, wo_h, out_h,
    frames_v, cot_v, ws_v, wt_v, gain_v, wq_v, wk_v, wv_v, wo_v, out_v,
    halo_v, ghalo_v, gnat_v, acc0, acc1, acc2,
    fc_s, sp_s, sg_s, tg_s, fc_r, sp_r, sg_r, tg_r,
    load_sem, out_sem, hs_sem, hr_sem, s_sem, r_sem,
):
    me = lax.axis_index("tm")
    sp = lax.axis_index("space")
    z, y = me // 8, lax.rem(me, 8)
    up, down = lax.rem(sp + 7, 8), lax.rem(sp + 1, 8)

    def peer(i):
        d = i + 1
        return lax.rem(z + d // 8, 8) * 8 + lax.rem(y + lax.rem(d, 8), 8)

    pairs = [
        (frames_h, frames_v), (ws_h, ws_v), (cot_h, cot_v), (wt_h, wt_v), (gain_h, gain_v),
        (wq_h, wq_v), (wk_h, wk_v), (wv_h, wv_v), (wo_h, wo_v),
    ]
    loads = [pltpu.make_async_copy(a, b, load_sem.at[i]) for i, (a, b) in enumerate(pairs)]
    for copy in loads:
        copy.start()

    barrier = pltpu.get_barrier_semaphore()
    for other in (up, down):
        pl.semaphore_signal(barrier, inc=1, device_id=(me, other), device_id_type=MESH)

    def greet(i, carry):
        pl.semaphore_signal(barrier, inc=1, device_id=(peer(i), sp), device_id_type=MESH)
        return carry

    lax.fori_loop(0, 63, greet, 0)

    def halo_copies(src, dst, k):
        return [
            pltpu.make_async_remote_copy(
                src.at[:, row], dst.at[side], hs_sem.at[k + side], hr_sem.at[k + side],
                device_id=(me, other), device_id_type=MESH,
            )
            for side, (row, other) in enumerate(((3, down), (0, up)))
        ]

    def send_all(src, dst, k):
        def go(i, carry):
            p = peer(i)
            pltpu.make_async_remote_copy(
                src.at[p], dst.at[me], s_sem.at[k], r_sem.at[k],
                device_id=(p, sp), device_id_type=MESH,
            ).start()
            return carry

        lax.fori_loop(0, 63, go, 0)
        dst[me] = src[me]

    def wait_all(dst, sem):
        pltpu.make_async_copy(dst.at[pl.ds(0, 63)], dst.at[pl.ds(0, 63)], sem).wait()

    row_m, col_n = iota((T, T), 0), iota((T, T), 1)
    natural = (row_m // 4) % 2 * 256 + row_m // 8 * 4 + row_m % 4
    to_message = (natural == col_n).astype(F32).astype(BF)

    def taps(src, weight, pick):
        for col_tap, acc in enumerate((acc0, acc1, acc2)):
            for f in range(2):
                x = src[f].reshape(256, C)
                acc[f] = pick(x, weight, 1, col_tap)
                acc[f, 64:256] += pick(x[0:192], weight, 0, col_tap)
                acc[f, 0:192] += pick(x[64:256], weight, 2, col_tap)

    def edges(halo, weight, pick):
        keep_up = jnp.where(sp > 0, 1.0, 0.0)
        keep_down = jnp.where(sp < 7, 1.0, 0.0)
        above = halo[0].reshape(128, C)
        below = halo[1].reshape(128, C)
        for col_tap, acc in enumerate((acc0, acc1, acc2)):
            first = pick(above, weight, 0, col_tap) * keep_up
            last = pick(below, weight, 2, col_tap) * keep_down
            for f in range(2):
                acc[f, 0:64] += first[f * 64 : f * 64 + 64]
                acc[f, 192:256] += last[f * 64 : f * 64 + 64]

    def columns():
        col = iota((T, C), 0) % 64
        before = jnp.where(col == 0, 0.0, roll_rows(acc0[...].reshape(T, C), 1))
        after = jnp.where(col == 63, 0.0, roll_rows(acc2[...].reshape(T, C), -1))
        return before + acc1[...].reshape(T, C) + after

    def pick_forward(x, weight, row_tap, col_tap):
        return mm(x, weight[row_tap, col_tap])

    def pick_backward(x, weight, row_tap, col_tap):
        return mm_nt(x, weight[2 - row_tap, 2 - col_tap])

    loads[0].wait()
    loads[1].wait()
    taps(frames_v, ws_v, pick_forward)

    pl.semaphore_wait(barrier, 65)
    halos = halo_copies(frames_v, halo_v, 0)
    for copy in halos:
        copy.start()
    fc_s[:, 0:16] = to_tiles(mm(to_message, frames_v[...].reshape(T, C)))
    loads[2].wait()
    fc_s[:, 16:32] = to_tiles(mm(to_message, cot_v[...].reshape(T, C)))
    for copy in halos:
        copy.wait()
    edges(halo_v, ws_v, pick_forward)
    spatial = columns().astype(BF)
    sp_s[...] = to_tiles(mm(to_message, spatial))
    send_all(sp_s, sp_r, 1)
    send_all(fc_s, fc_r, 0)
    for copy in loads[3:]:
        copy.wait()

    wait_all(fc_r, r_sem.at[0])
    by_pixel = (row_m % 128 * 4 + row_m // 128 == col_n).astype(F32).astype(BF)
    cot_n = from_tiles(fc_r[:, 16:32]).astype(BF)
    cot_p = mm(by_pixel, cot_n).astype(BF)
    out_grad = mm_nt(cot_p, wo_v[...]).astype(BF)
    frames_n = from_tiles(fc_r[:, 0:16])
    wait_all(sp_r, r_sem.at[1])
    spatial_n = from_tiles(sp_r[...]).astype(BF)
    token = iota((T, C), 0)
    hidden_n = (
        frames_n
        + mm(spatial_n, wt_v[0])
        + jnp.where(token < 4, 0.0, roll_rows(mm(spatial_n, wt_v[1]), 4))
        + jnp.where(token < 8, 0.0, roll_rows(mm(spatial_n, wt_v[2]), 8))
    ).astype(BF)
    hidden = mm(by_pixel, hidden_n)
    gain = gain_v[...]
    inverse = lax.rsqrt(jnp.mean(hidden * hidden, axis=-1, keepdims=True) + EPSILON)
    normed = (hidden * inverse * gain).astype(BF)
    query = mm(normed, wq_v[...]).astype(BF)
    key = mm(normed, wk_v[...]).astype(BF)
    value = mm(normed, wv_v[...]).astype(BF)
    scale = 1.0 / 16.0
    causal = iota((128, 128), 1) <= iota((128, 128), 0)
    dq, dk, dv = [], [], []
    for p in range(4):
        rows = slice(p * 128, p * 128 + 128)
        q, k, v, g = query[rows], key[rows], value[rows], out_grad[rows]
        weights = jnp.where(causal, jnp.exp(mm_nt(q, k) * scale), 0.0)
        probs = weights / jnp.sum(weights, axis=-1, keepdims=True)
        prob_grad = mm_nt(g, v)
        centre = jnp.sum(probs * prob_grad, axis=-1, keepdims=True)
        score_grad = (probs * (prob_grad - centre) * scale).astype(BF)
        dv.append(mm_tn(probs.astype(BF), g).astype(BF))
        dq.append(mm(score_grad, k).astype(BF))
        dk.append(mm_tn(score_grad, q).astype(BF))
    normed_grad = (
        mm_nt(jnp.concatenate(dq, 0), wq_v[...])
        + mm_nt(jnp.concatenate(dk, 0), wk_v[...])
        + mm_nt(jnp.concatenate(dv, 0), wv_v[...])
    )
    scaled = normed_grad * gain
    mean = jnp.mean(hidden * scaled, axis=-1, keepdims=True)
    attn_grad = (inverse * scaled - hidden * (inverse * inverse * inverse) * mean).astype(BF)
    total_p = (cot_p.astype(F32) + attn_grad.astype(F32)).astype(BF)
    total_f = mm_tn(by_pixel, total_p)
    total_n = total_f.astype(BF)
    sgrad = (
        mm_nt(total_n, wt_v[0])
        + jnp.where(token >= T - 4, 0.0, roll_rows(mm_nt(total_n, wt_v[1]), -4))
        + jnp.where(token >= T - 8, 0.0, roll_rows(mm_nt(total_n, wt_v[2]), -8))
    )
    sg_s[...] = to_tiles(sgrad)
    send_all(sg_s, sg_r, 2)
    tg_s[...] = to_tiles(total_f)
    send_all(tg_s, tg_r, 3)

    wait_all(sg_r, r_sem.at[2])
    gnat_v[...] = mm_tn(to_message, from_tiles(sg_r[...]).astype(BF)).astype(BF).reshape(2, 4, 64, C)
    ghalos = halo_copies(gnat_v, ghalo_v, 2)
    for copy in ghalos:
        copy.start()
    taps(gnat_v, ws_v, pick_backward)
    for copy in ghalos:
        copy.wait()
    edges(ghalo_v, ws_v, pick_backward)
    wait_all(tg_r, r_sem.at[3])
    total = mm_tn(to_message, from_tiles(tg_r[...]).astype(BF))
    out_v[...] = (total + columns()).astype(BF).reshape(2, 4, 64, C)
    done = pltpu.make_async_copy(out_v, out_h, out_sem)
    done.start()
    for k, src in enumerate((fc_s, sp_s, sg_s, tg_s)):
        wait_all(src, s_sem.at[k])
    done.wait()


def body(frames, cotangent, w_spatial, w_temporal, norm_gain, w_query, w_key, w_value, w_out):
    big = (2, 4, 64, C)
    square = (C, C)
    vmem = pltpu.VMEM
    dma = pltpu.SemaphoreType.DMA
    message = vmem((64, 16, 128), BF)
    double = vmem((64, 32, 128), BF)
    return pl.pallas_call(
        kernel,
        out_shape=jax.ShapeDtypeStruct(big, BF),
        in_specs=[pl.BlockSpec(memory_space=pl.ANY)] * 9,
        out_specs=pl.BlockSpec(memory_space=pl.ANY),
        scratch_shapes=[
            vmem(big, BF), vmem(big, BF), vmem((3, 3, C, C), BF), vmem((3, C, C), BF), vmem((1, C), F32),
            vmem(square, BF), vmem(square, BF), vmem(square, BF), vmem(square, BF), vmem(big, BF),
            vmem((2, 2, 64, C), BF), vmem((2, 2, 64, C), BF), vmem(big, BF),
            vmem((2, 256, C), F32), vmem((2, 256, C), F32), vmem((2, 256, C), F32),
            double, message, message, message, double, message, message, message,
            dma((9,)), dma, dma((4,)), dma((4,)), dma((4,)), dma((4,)),
        ],
        compiler_params=pltpu.CompilerParams(
            collective_id=0, has_side_effects=True, vmem_limit_bytes=60 * 1024 * 1024
        ),
        name="whole",
    )(frames, cotangent, w_spatial, w_temporal, norm_gain.reshape(1, C), w_query, w_key, w_value, w_out)


def solution(mesh):
    return jax.shard_map(
        body,
        mesh=mesh,
        in_specs=(
            P("tm", "space", None, None),
            P("tm", "space", None, None),
            P(),
            P(),
            P(),
            P(),
            P(),
            P(),
            P(),
        ),
        out_specs=P("tm", "space", None, None),
        check_vma=False,
    )
```

```python
import jax
import jax.numpy as jnp
from jax import lax
from jax.experimental import pallas as pl
from jax.experimental.pallas import tpu as pltpu
from jax.sharding import PartitionSpec as P

EPSILON = 1e-05
MESH = pl.DeviceIdType.MESH
BF = jnp.bfloat16
F32 = jnp.float32
T = 512
C = 256


def mm(a, b):
    return jnp.dot(a, b, preferred_element_type=F32)


def mm_nt(a, b):
    return lax.dot_general(a, b, (((1,), (1,)), ((), ())), preferred_element_type=F32)


def mm_tn(a, b):
    return lax.dot_general(a, b, (((0,), (0,)), ((), ())), preferred_element_type=F32)


def iota(shape, dim):
    return lax.broadcasted_iota(jnp.int32, shape, dim)


def to_tiles(x):
    x = x.reshape(64, 8, C)
    return jnp.concatenate([x[:, :, :128], x[:, :, 128:]], axis=1).astype(BF)


def from_tiles(x):
    x = x.astype(F32)
    return jnp.concatenate([x[:, :8], x[:, 8:]], axis=2).reshape(T, C)


def roll_rows(x, distance):
    return pltpu.roll(x, distance % x.shape[0], 0)


def kernel(
    frames_h, cot_h, ws_h, wt_h, gain_h, wq_h, wk_h, wv_h, wo_h, out_v,
    frames_v, cot_v, ws_v, wt_v, gain_v, wq_v, wk_v, wv_v, wo_v,
    halo_v, ghalo_v, gnat_v, acc0, acc1, acc2,
    fc_s, sp_s, sg_s, tg_s, fc_r, sp_r, sg_r, tg_r,
    load_sem, hs_sem, hr_sem, s_sem, r_sem, before_sem, row_sem,
):
    me = lax.axis_index("tm")
    sp = lax.axis_index("space")
    z, y = me // 8, lax.rem(me, 8)
    up, down = lax.rem(sp + 7, 8), lax.rem(sp + 1, 8)

    pairs = [
        (frames_h, frames_v), (cot_h, cot_v), (ws_h, ws_v), (wt_h, wt_v), (gain_h, gain_v),
        (wq_h, wq_v), (wk_h, wk_v), (wv_h, wv_v), (wo_h, wo_v),
    ]
    loads = [pltpu.make_async_copy(a, b, load_sem.at[i]) for i, (a, b) in enumerate(pairs)]

    barrier = pltpu.get_barrier_semaphore()
    for other in (up, down):
        pl.semaphore_signal(barrier, inc=1, device_id=(me, other), device_id_type=MESH)

    @pl.when(z > 0)
    def _():
        pl.semaphore_signal(barrier, inc=1, device_id=(me - 8, sp), device_id_type=MESH)

    for j in range(1, 8):
        p = z * 8 + lax.rem(y + j, 8)
        pl.semaphore_signal(barrier, inc=1, device_id=(p, sp), device_id_type=MESH)

    @pl.when(z < 7)
    def _():
        pl.semaphore_signal(barrier, inc=1, device_id=(me + 8, sp), device_id_type=MESH)

    for copy in loads:
        copy.start()

    def halo_copies(src, dst, k):
        return [
            pltpu.make_async_remote_copy(
                src.at[:, row], dst.at[side], hs_sem.at[k + side], hr_sem.at[k + side],
                device_id=(me, other), device_id_type=MESH,
            )
            for side, (row, other) in enumerate(((3, down), (0, up)))
        ]

    def send_row(src, dst, k, row, others=8):
        for j in range(8 - others, 8):
            p = row * 8 + lax.rem(y + j, 8)
            pltpu.make_async_remote_copy(
                src.at[p], dst.at[me], s_sem.at[k], r_sem.at[k],
                device_id=(p, sp), device_id_type=MESH,
            ).start()

    def send_before(src, dst, k):
        send_row(src, dst, k, z, 7)

        def go(i, carry):
            send_row(src, dst, k, z - i)
            return carry

        lax.fori_loop(1, z + 1, go, 0)
        dst[me] = src[me]

    def send_all(src, dst, k):
        def go(i, carry):
            send_row(src, dst, k, lax.rem(z + i, 8))
            return carry

        lax.fori_loop(1, 8, go, 0)
        send_row(src, dst, k, z, 7)
        dst[me] = src[me]

    def wait_all(dst, sem):
        pltpu.make_async_copy(dst.at[pl.ds(0, 63)], dst.at[pl.ds(0, 63)], sem).wait()

    row_m, col_n = iota((T, T), 0), iota((T, T), 1)
    natural = (row_m // 4) % 2 * 256 + row_m // 8 * 4 + row_m % 4
    to_message = (natural == col_n).astype(F32).astype(BF)

    def taps(src, weight, pick):
        for col_tap, acc in enumerate((acc0, acc1, acc2)):
            for f in range(2):
                x = src[f].reshape(256, C)
                acc[f] = pick(x, weight, 1, col_tap)
                acc[f, 64:256] += pick(x[0:192], weight, 0, col_tap)
                acc[f, 0:192] += pick(x[64:256], weight, 2, col_tap)

    def edges(halo, weight, pick):
        keep_up = jnp.where(sp > 0, 1.0, 0.0)
        keep_down = jnp.where(sp < 7, 1.0, 0.0)
        above = halo[0].reshape(128, C)
        below = halo[1].reshape(128, C)
        for col_tap, acc in enumerate((acc0, acc1, acc2)):
            first = pick(above, weight, 0, col_tap) * keep_up
            last = pick(below, weight, 2, col_tap) * keep_down
            for f in range(2):
                acc[f, 0:64] += first[f * 64 : f * 64 + 64]
                acc[f, 192:256] += last[f * 64 : f * 64 + 64]

    def columns():
        col = iota((T, C), 0) % 64
        before = jnp.where(col == 0, 0.0, roll_rows(acc0[...].reshape(T, C), 1))
        after = jnp.where(col == 63, 0.0, roll_rows(acc2[...].reshape(T, C), -1))
        return before + acc1[...].reshape(T, C) + after

    def pick_forward(x, weight, row_tap, col_tap):
        return mm(x, weight[row_tap, col_tap])

    def pick_backward(x, weight, row_tap, col_tap):
        return mm_nt(x, weight[2 - row_tap, 2 - col_tap])

    met = 9 + jnp.where(z > 0, 1, 0) + jnp.where(z < 7, 1, 0)
    pl.semaphore_wait(barrier, met)
    halos = halo_copies(frames_h, halo_v, 0)
    for copy in halos:
        copy.start()

    @pl.when(z > 0)
    def _():
        pl.semaphore_wait(before_sem, 1)

    @pl.when(z < 7)
    def _():
        pl.semaphore_signal(before_sem, inc=1, device_id=(me + 8, sp), device_id_type=MESH)

    def tell(i, carry):
        pl.semaphore_signal(
            row_sem.at[z], inc=1, device_id=((z - i) * 8 + y, sp), device_id_type=MESH
        )
        return carry

    lax.fori_loop(1, z + 1, tell, 0)

    loads[0].wait()
    fc_s[:, 0:16] = to_tiles(mm(to_message, frames_v[...].reshape(T, C)))
    loads[1].wait()
    fc_s[:, 16:32] = to_tiles(mm(to_message, cot_v[...].reshape(T, C)))
    send_before(fc_s, fc_r, 0)
    loads[2].wait()
    taps(frames_v, ws_v, pick_forward)
    for copy in halos:
        copy.wait()
    edges(halo_v, ws_v, pick_forward)
    spatial = columns().astype(BF)
    sp_s[...] = to_tiles(mm(to_message, spatial))
    send_before(sp_s, sp_r, 1)

    def later(row, carry):
        pl.semaphore_wait(row_sem.at[row], 1)
        send_row(fc_s, fc_r, 0, row)
        send_row(sp_s, sp_r, 1, row)
        return carry

    lax.fori_loop(z + 1, 8, later, 0)
    for copy in loads[3:]:
        copy.wait()

    wait_all(fc_r, r_sem.at[0])
    by_pixel = (row_m % 128 * 4 + row_m // 128 == col_n).astype(F32).astype(BF)
    cot_n = from_tiles(fc_r[:, 16:32]).astype(BF)
    cot_p = mm(by_pixel, cot_n).astype(BF)
    out_grad = mm_nt(cot_p, wo_v[...]).astype(BF)
    frames_n = from_tiles(fc_r[:, 0:16])
    wait_all(sp_r, r_sem.at[1])
    spatial_n = from_tiles(sp_r[...]).astype(BF)
    token = iota((T, C), 0)
    hidden_n = (
        frames_n
        + mm(spatial_n, wt_v[0])
        + jnp.where(token < 4, 0.0, roll_rows(mm(spatial_n, wt_v[1]), 4))
        + jnp.where(token < 8, 0.0, roll_rows(mm(spatial_n, wt_v[2]), 8))
    ).astype(BF)
    hidden = mm(by_pixel, hidden_n)
    gain = gain_v[...]
    inverse = lax.rsqrt(jnp.mean(hidden * hidden, axis=-1, keepdims=True) + EPSILON)
    normed = (hidden * inverse * gain).astype(BF)
    query = mm(normed, wq_v[...]).astype(BF)
    key = mm(normed, wk_v[...]).astype(BF)
    value = mm(normed, wv_v[...]).astype(BF)
    scale = 1.0 / 16.0
    causal = iota((128, 128), 1) <= iota((128, 128), 0)
    dq, dk, dv = [], [], []
    for p in range(4):
        rows = slice(p * 128, p * 128 + 128)
        q, k, v, g = query[rows], key[rows], value[rows], out_grad[rows]
        weights = jnp.where(causal, jnp.exp(mm_nt(q, k) * scale), 0.0)
        probs = weights / jnp.sum(weights, axis=-1, keepdims=True)
        prob_grad = mm_nt(g, v)
        centre = jnp.sum(probs * prob_grad, axis=-1, keepdims=True)
        score_grad = (probs * (prob_grad - centre) * scale).astype(BF)
        dv.append(mm_tn(probs.astype(BF), g).astype(BF))
        dq.append(mm(score_grad, k).astype(BF))
        dk.append(mm_tn(score_grad, q).astype(BF))
    normed_grad = (
        mm_nt(jnp.concatenate(dq, 0), wq_v[...])
        + mm_nt(jnp.concatenate(dk, 0), wk_v[...])
        + mm_nt(jnp.concatenate(dv, 0), wv_v[...])
    )
    scaled = normed_grad * gain
    mean = jnp.mean(hidden * scaled, axis=-1, keepdims=True)
    attn_grad = (inverse * scaled - hidden * (inverse * inverse * inverse) * mean).astype(BF)
    total_p = (cot_p.astype(F32) + attn_grad.astype(F32)).astype(BF)
    total_f = mm_tn(by_pixel, total_p)
    total_n = total_f.astype(BF)
    sgrad = (
        mm_nt(total_n, wt_v[0])
        + jnp.where(token >= T - 4, 0.0, roll_rows(mm_nt(total_n, wt_v[1]), -4))
        + jnp.where(token >= T - 8, 0.0, roll_rows(mm_nt(total_n, wt_v[2]), -8))
    )
    sg_s[...] = to_tiles(sgrad)
    send_all(sg_s, sg_r, 2)
    tg_s[...] = to_tiles(total_f)
    wait_all(sg_s, s_sem.at[2])
    send_all(tg_s, tg_r, 3)

    wait_all(sg_r, r_sem.at[2])
    gnat_v[...] = mm_tn(to_message, from_tiles(sg_r[...]).astype(BF)).astype(BF).reshape(2, 4, 64, C)
    ghalos = halo_copies(gnat_v, ghalo_v, 2)
    for copy in ghalos:
        copy.start()
    taps(gnat_v, ws_v, pick_backward)
    for copy in ghalos:
        copy.wait()
    edges(ghalo_v, ws_v, pick_backward)
    wait_all(tg_r, r_sem.at[3])
    total = mm_tn(to_message, from_tiles(tg_r[...]).astype(BF))
    out_v[...] = (total + columns()).astype(BF).reshape(2, 4, 64, C)
    for k, src in ((0, fc_s), (1, sp_s), (3, tg_s)):
        wait_all(src, s_sem.at[k])


def body(frames, cotangent, w_spatial, w_temporal, norm_gain, w_query, w_key, w_value, w_out):
    big = (2, 4, 64, C)
    square = (C, C)
    vmem = pltpu.VMEM
    dma = pltpu.SemaphoreType.DMA
    message = vmem((64, 16, 128), BF)
    double = vmem((64, 32, 128), BF)
    return pl.pallas_call(
        kernel,
        out_shape=jax.ShapeDtypeStruct(big, BF),
        in_specs=[pl.BlockSpec(memory_space=pl.ANY)] * 9,
        out_specs=pl.BlockSpec(memory_space=pltpu.VMEM),
        scratch_shapes=[
            vmem(big, BF), vmem(big, BF), vmem((3, 3, C, C), BF), vmem((3, C, C), BF), vmem((1, C), F32),
            vmem(square, BF), vmem(square, BF), vmem(square, BF), vmem(square, BF),
            vmem((2, 2, 64, C), BF), vmem((2, 2, 64, C), BF), vmem(big, BF),
            vmem((2, 256, C), F32), vmem((2, 256, C), F32), vmem((2, 256, C), F32),
            double, message, message, message, double, message, message, message,
            dma((9,)), dma((4,)), dma((4,)), dma((4,)), dma((4,)),
            pltpu.SemaphoreType.REGULAR, pltpu.SemaphoreType.REGULAR((8,)),
        ],
        compiler_params=pltpu.CompilerParams(
            collective_id=0, has_side_effects=True, vmem_limit_bytes=56 * 1024 * 1024
        ),
        name="whole",
    )(frames, cotangent, w_spatial, w_temporal, norm_gain.reshape(1, C), w_query, w_key, w_value, w_out)


def solution(mesh):
    return jax.shard_map(
        body,
        mesh=mesh,
        in_specs=(
            P("tm", "space", None, None),
            P("tm", "space", None, None),
            P(),
            P(),
            P(),
            P(),
            P(),
            P(),
            P(),
        ),
        out_specs=P("tm", "space", None, None),
        check_vma=False,
    )
```

```python
import jax
import jax.numpy as jnp
from jax import lax
from jax.experimental import pallas as pl
from jax.experimental.pallas import tpu as pltpu
from jax.sharding import PartitionSpec as P

EPSILON = 1e-05
MESH = pl.DeviceIdType.MESH
BF = jnp.bfloat16
F32 = jnp.float32
T = 512
C = 256


def mm(a, b):
    return jnp.dot(a, b, preferred_element_type=F32)


def mm_nt(a, b):
    return lax.dot_general(a, b, (((1,), (1,)), ((), ())), preferred_element_type=F32)


def mm_tn(a, b):
    return lax.dot_general(a, b, (((0,), (0,)), ((), ())), preferred_element_type=F32)


def iota(shape, dim):
    return lax.broadcasted_iota(jnp.int32, shape, dim)


def to_tiles(x):
    x = x.reshape(64, 8, C)
    return jnp.concatenate([x[:, :, :128], x[:, :, 128:]], axis=1).astype(BF)


def from_tiles(x):
    x = x.astype(F32)
    return jnp.concatenate([x[:, :8], x[:, 8:]], axis=2).reshape(T, C)


def roll_rows(x, distance):
    return pltpu.roll(x, distance % x.shape[0], 0)


def kernel(
    frames_h, cot_h, ws_h, wt_h, gain_h, wq_h, wk_h, wv_h, wo_h, out_v,
    frames_v, cot_v, ws_v, wt_v, gain_v, wq_v, wk_v, wv_v, wo_v,
    halo_v, ghalo_v, gnat_v, spat_v, prev_v, acc0, acc1, acc2,
    ct_s, hd_s, sg_s, tg_s, ct_r, hd_r, sg_r, tg_r,
    load_sem, hs_sem, hr_sem, s_sem, r_sem, fs_sem, fr_sem, before_sem, row_sem,
):
    me = lax.axis_index("tm")
    sp = lax.axis_index("space")
    z, y = me // 8, lax.rem(me, 8)
    up, down = lax.rem(sp + 7, 8), lax.rem(sp + 1, 8)

    pairs = [
        (frames_h, frames_v), (cot_h, cot_v), (ws_h, ws_v), (wt_h, wt_v), (gain_h, gain_v),
        (wq_h, wq_v), (wk_h, wk_v), (wv_h, wv_v), (wo_h, wo_v),
    ]
    loads = [pltpu.make_async_copy(a, b, load_sem.at[i]) for i, (a, b) in enumerate(pairs)]

    barrier = pltpu.get_barrier_semaphore()
    for other in (up, down):
        pl.semaphore_signal(barrier, inc=1, device_id=(me, other), device_id_type=MESH)

    @pl.when(z > 0)
    def _():
        pl.semaphore_signal(barrier, inc=1, device_id=(me - 8, sp), device_id_type=MESH)

    for j in range(1, 8):
        p = z * 8 + lax.rem(y + j, 8)
        pl.semaphore_signal(barrier, inc=1, device_id=(p, sp), device_id_type=MESH)

    @pl.when(z < 7)
    def _():
        pl.semaphore_signal(barrier, inc=1, device_id=(me + 8, sp), device_id_type=MESH)

    @pl.when(jnp.logical_and(y == 0, z > 0))
    def _():
        pl.semaphore_signal(barrier, inc=1, device_id=(me - 1, sp), device_id_type=MESH)

    for copy in loads:
        copy.start()

    def halo_copies(src, dst, k):
        return [
            pltpu.make_async_remote_copy(
                src.at[:, row], dst.at[side], hs_sem.at[k + side], hr_sem.at[k + side],
                device_id=(me, other), device_id_type=MESH,
            )
            for side, (row, other) in enumerate(((3, down), (0, up)))
        ]

    def send_row(src, dst, k, row, others=8):
        for j in range(8 - others, 8):
            p = row * 8 + lax.rem(y + j, 8)
            pltpu.make_async_remote_copy(
                src.at[p], dst.at[me], s_sem.at[k], r_sem.at[k],
                device_id=(p, sp), device_id_type=MESH,
            ).start()

    def send_before(src, dst, k):
        send_row(src, dst, k, z, 7)

        def go(i, carry):
            send_row(src, dst, k, z - i)
            return carry

        lax.fori_loop(1, z + 1, go, 0)
        dst[me] = src[me]

    def send_all(src, dst, k):
        def go(i, carry):
            send_row(src, dst, k, lax.rem(z + i, 8))
            return carry

        lax.fori_loop(1, 8, go, 0)
        send_row(src, dst, k, z, 7)
        dst[me] = src[me]

    def send_ascending(src, dst, k):
        def go(i, carry):
            send_row(src, dst, k, i)
            return carry

        lax.fori_loop(0, z, go, 0)
        send_row(src, dst, k, z, 7)
        lax.fori_loop(z + 1, 8, go, 0)
        dst[me] = src[me]

    def wait_all(dst, sem):
        pltpu.make_async_copy(dst.at[pl.ds(0, 63)], dst.at[pl.ds(0, 63)], sem).wait()

    row_m, col_n = iota((T, T), 0), iota((T, T), 1)
    natural = (row_m // 4) % 2 * 256 + row_m // 8 * 4 + row_m % 4
    to_message = (natural == col_n).astype(F32).astype(BF)

    def taps(src, weight, pick):
        for col_tap, acc in enumerate((acc0, acc1, acc2)):
            for f in range(2):
                x = src[f].reshape(256, C)
                acc[f] = pick(x, weight, 1, col_tap)
                acc[f, 64:256] += pick(x[0:192], weight, 0, col_tap)
                acc[f, 0:192] += pick(x[64:256], weight, 2, col_tap)

    def edges(halo, weight, pick):
        keep_up = jnp.where(sp > 0, 1.0, 0.0)
        keep_down = jnp.where(sp < 7, 1.0, 0.0)
        above = halo[0].reshape(128, C)
        below = halo[1].reshape(128, C)
        for col_tap, acc in enumerate((acc0, acc1, acc2)):
            first = pick(above, weight, 0, col_tap) * keep_up
            last = pick(below, weight, 2, col_tap) * keep_down
            for f in range(2):
                acc[f, 0:64] += first[f * 64 : f * 64 + 64]
                acc[f, 192:256] += last[f * 64 : f * 64 + 64]

    def columns(f, low, high):
        rows = slice(low * 64, high * 64)
        col = iota(((high - low) * 64, C), 0) % 64
        before = jnp.where(col == 0, 0.0, roll_rows(acc0[f, rows], 1))
        after = jnp.where(col == 63, 0.0, roll_rows(acc2[f, rows], -1))
        return before + acc1[f, rows] + after

    def pick_forward(x, weight, row_tap, col_tap):
        return mm(x, weight[row_tap, col_tap])

    def pick_backward(x, weight, row_tap, col_tap):
        return mm_nt(x, weight[2 - row_tap, 2 - col_tap])

    met = 9 + jnp.where(z > 0, 1, 0) + jnp.where(z < 7, 1, 0)
    met += jnp.where(jnp.logical_and(y == 7, z < 7), 1, 0)
    pl.semaphore_wait(barrier, met)
    halos = halo_copies(frames_h, halo_v, 0)
    for copy in halos:
        copy.start()

    def frame_copy(part, rows):
        return pltpu.make_async_remote_copy(
            spat_v.at[:, rows], prev_v.at[:, rows], fs_sem.at[part], fr_sem.at[part],
            device_id=(me + 1, sp), device_id_type=MESH,
        )

    shifts = [frame_copy(0, pl.ds(1, 2)), frame_copy(1, pl.ds(0, 1)), frame_copy(2, pl.ds(3, 1))]

    def spatial_rows(low, high):
        for f in range(2):
            rows = columns(f, low, high).astype(BF)
            spat_v[f, low:high] = rows.reshape(high - low, 64, C)

    loads[0].wait()
    loads[2].wait()
    taps(frames_v, ws_v, pick_forward)
    spatial_rows(1, 3)

    @pl.when(me < 63)
    def _():
        shifts[0].start()

    @pl.when(z > 0)
    def _():
        pl.semaphore_wait(before_sem, 1)

    @pl.when(z < 7)
    def _():
        pl.semaphore_signal(before_sem, inc=1, device_id=(me + 8, sp), device_id_type=MESH)

    def tell(i, carry):
        pl.semaphore_signal(
            row_sem.at[z], inc=1, device_id=((z - i) * 8 + y, sp), device_id_type=MESH
        )
        return carry

    lax.fori_loop(1, z + 1, tell, 0)

    for copy in halos:
        copy.wait()
    edges(halo_v, ws_v, pick_forward)
    spatial_rows(0, 1)
    spatial_rows(3, 4)

    @pl.when(me < 63)
    def _():
        shifts[1].start()
        shifts[2].start()

    loads[1].wait()
    ct_s[...] = to_tiles(mm(to_message, cot_v[...].reshape(T, C)))
    send_before(ct_s, ct_r, 0)
    for copy in loads[3:]:
        copy.wait()
    now = [spat_v[f].reshape(256, C) for f in range(2)]
    acc0[0] = frames_v[0].reshape(256, C).astype(F32) + mm(now[0], wt_v[0])
    acc0[1] = frames_v[1].reshape(256, C).astype(F32) + mm(now[1], wt_v[0]) + mm(now[0], wt_v[1])
    def later_cot(row, carry):
        pl.semaphore_wait(row_sem.at[row], 1)
        send_row(ct_s, ct_r, 0, row)
        return carry

    lax.fori_loop(z + 1, 8, later_cot, 0)

    @pl.when(me > 0)
    def _():
        for copy in shifts:
            copy.wait_recv()

    @pl.when(me == 0)
    def _():
        prev_v[...] = jnp.zeros_like(prev_v)

    past = [prev_v[f].reshape(256, C) for f in range(2)]
    acc0[0] += mm(past[1], wt_v[1]) + mm(past[0], wt_v[2])
    acc0[1] += mm(past[1], wt_v[2])
    hd_s[...] = to_tiles(mm(to_message, acc0[...].reshape(T, C).astype(BF)))
    send_before(hd_s, hd_r, 1)

    def later(row, carry):
        send_row(hd_s, hd_r, 1, row)
        return carry

    lax.fori_loop(z + 1, 8, later, 0)

    wait_all(ct_r, r_sem.at[0])
    by_pixel = (row_m % 128 * 4 + row_m // 128 == col_n).astype(F32).astype(BF)
    cot_n = from_tiles(ct_r[...]).astype(BF)
    cot_p = mm(by_pixel, cot_n).astype(BF)
    out_grad = mm_nt(cot_p, wo_v[...]).astype(BF)
    wait_all(hd_r, r_sem.at[1])
    token = iota((T, C), 0)
    hidden = mm(by_pixel, from_tiles(hd_r[...]).astype(BF))
    gain = gain_v[...]
    inverse = lax.rsqrt(jnp.mean(hidden * hidden, axis=-1, keepdims=True) + EPSILON)
    normed = (hidden * inverse * gain).astype(BF)
    query = mm(normed, wq_v[...]).astype(BF)
    key = mm(normed, wk_v[...]).astype(BF)
    value = mm(normed, wv_v[...]).astype(BF)
    scale = 1.0 / 16.0
    causal = iota((128, 128), 1) <= iota((128, 128), 0)
    dq, dk, dv = [], [], []
    for p in range(4):
        rows = slice(p * 128, p * 128 + 128)
        q, k, v, g = query[rows], key[rows], value[rows], out_grad[rows]
        weights = jnp.where(causal, jnp.exp(mm_nt(q, k) * scale), 0.0)
        probs = weights / jnp.sum(weights, axis=-1, keepdims=True)
        prob_grad = mm_nt(g, v)
        centre = jnp.sum(probs * prob_grad, axis=-1, keepdims=True)
        score_grad = (probs * (prob_grad - centre) * scale).astype(BF)
        dv.append(mm_tn(probs.astype(BF), g).astype(BF))
        dq.append(mm(score_grad, k).astype(BF))
        dk.append(mm_tn(score_grad, q).astype(BF))
    normed_grad = (
        mm_nt(jnp.concatenate(dq, 0), wq_v[...])
        + mm_nt(jnp.concatenate(dk, 0), wk_v[...])
        + mm_nt(jnp.concatenate(dv, 0), wv_v[...])
    )
    scaled = normed_grad * gain
    mean = jnp.mean(hidden * scaled, axis=-1, keepdims=True)
    attn_grad = (inverse * scaled - hidden * (inverse * inverse * inverse) * mean).astype(BF)
    total_p = (cot_p.astype(F32) + attn_grad.astype(F32)).astype(BF)
    total_f = mm_tn(by_pixel, total_p)
    total_n = total_f.astype(BF)
    sgrad = (
        mm_nt(total_n, wt_v[0])
        + jnp.where(token >= T - 4, 0.0, roll_rows(mm_nt(total_n, wt_v[1]), -4))
        + jnp.where(token >= T - 8, 0.0, roll_rows(mm_nt(total_n, wt_v[2]), -8))
    )
    sg_s[...] = to_tiles(sgrad)
    send_ascending(sg_s, sg_r, 2)
    tg_s[...] = to_tiles(total_f)
    wait_all(sg_s, s_sem.at[2])
    send_ascending(tg_s, tg_r, 3)

    wait_all(sg_r, r_sem.at[2])
    gnat_v[...] = mm_tn(to_message, from_tiles(sg_r[...]).astype(BF)).astype(BF).reshape(2, 4, 64, C)
    ghalos = halo_copies(gnat_v, ghalo_v, 2)
    for copy in ghalos:
        copy.start()
    taps(gnat_v, ws_v, pick_backward)
    for copy in ghalos:
        copy.wait()
    edges(ghalo_v, ws_v, pick_backward)
    wait_all(tg_r, r_sem.at[3])
    total = mm_tn(to_message, from_tiles(tg_r[...]).astype(BF))
    for f in range(2):
        out_v[f] = (total[f * 256 : f * 256 + 256] + columns(f, 0, 4)).astype(BF).reshape(4, 64, C)

    @pl.when(me < 63)
    def _():
        for copy in shifts:
            copy.wait_send()

    for k, src in ((0, ct_s), (1, hd_s), (3, tg_s)):
        wait_all(src, s_sem.at[k])


def body(frames, cotangent, w_spatial, w_temporal, norm_gain, w_query, w_key, w_value, w_out):
    big = (2, 4, 64, C)
    square = (C, C)
    vmem = pltpu.VMEM
    dma = pltpu.SemaphoreType.DMA
    message = vmem((64, 16, 128), BF)
    arrays = (frames, cotangent, w_spatial, w_temporal, norm_gain.reshape(1, C), w_query, w_key, w_value, w_out)
    arrays = [pltpu.with_memory_space_constraint(a, pltpu.HBM) for a in arrays]
    return pl.pallas_call(
        kernel,
        out_shape=jax.ShapeDtypeStruct(big, BF),
        in_specs=[pl.BlockSpec(memory_space=pl.ANY)] * 9,
        out_specs=pl.BlockSpec(memory_space=pltpu.VMEM),
        scratch_shapes=[
            vmem(big, BF), vmem(big, BF), vmem((3, 3, C, C), BF), vmem((3, C, C), BF), vmem((1, C), F32),
            vmem(square, BF), vmem(square, BF), vmem(square, BF), vmem(square, BF),
            vmem((2, 2, 64, C), BF), vmem((2, 2, 64, C), BF), vmem(big, BF), vmem(big, BF), vmem(big, BF),
            vmem((2, 256, C), F32), vmem((2, 256, C), F32), vmem((2, 256, C), F32),
            message, message, message, message, message, message, message, message,
            dma((9,)), dma((4,)), dma((4,)), dma((4,)), dma((4,)), dma((3,)), dma((3,)),
            pltpu.SemaphoreType.REGULAR, pltpu.SemaphoreType.REGULAR((8,)),
        ],
        compiler_params=pltpu.CompilerParams(
            collective_id=0, has_side_effects=True, vmem_limit_bytes=48 * 1024 * 1024
        ),
        name="whole",
    )(*arrays)


def solution(mesh):
    return jax.shard_map(
        body,
        mesh=mesh,
        in_specs=(
            P("tm", "space", None, None),
            P("tm", "space", None, None),
            P(),
            P(),
            P(),
            P(),
            P(),
            P(),
            P(),
        ),
        out_specs=P("tm", "space", None, None),
        check_vma=False,
    )
```

```python
import jax
import jax.numpy as jnp
from jax import lax
from jax.experimental import pallas as pl
from jax.experimental.pallas import tpu as pltpu
from jax.sharding import PartitionSpec as P

EPSILON = 1e-05
MESH = pl.DeviceIdType.MESH
BF = jnp.bfloat16
F32 = jnp.float32
T = 512
C = 256


def mm(a, b):
    return jnp.dot(a, b, preferred_element_type=F32)


def mm_nt(a, b):
    return lax.dot_general(a, b, (((1,), (1,)), ((), ())), preferred_element_type=F32)


def mm_tn(a, b):
    return lax.dot_general(a, b, (((0,), (0,)), ((), ())), preferred_element_type=F32)


def iota(shape, dim):
    return lax.broadcasted_iota(jnp.int32, shape, dim)


def to_tiles(x):
    x = x.reshape(64, 8, C)
    return jnp.concatenate([x[:, :, :128], x[:, :, 128:]], axis=1).astype(BF)


def from_tiles(x):
    x = x.astype(F32)
    return jnp.concatenate([x[:, :8], x[:, 8:]], axis=2).reshape(T, C)


def roll_rows(x, distance):
    return pltpu.roll(x, distance % x.shape[0], 0)


def kernel(
    frames_h, cot_h, ws_h, wt_h, gain_h, wq_h, wk_h, wv_h, wo_h, out_v,
    frames_v, cot_v, ws_v, wt_v, gain_v, wq_v, wk_v, wv_v, wo_v,
    halo_v, ghalo_v, gnat_v, spat_v, prev_v, acc0, acc1, acc2,
    ct_s, hd_s, sg_s, tg_s, ct_r, hd_r, sg_r, tg_r, to_msg_v, from_msg_v, by_pixel_v, by_frame_v,
    load_sem, hs_sem, hr_sem, s_sem, r_sem, fs_sem, fr_sem, before_sem, row_sem,
):
    me = lax.axis_index("tm")
    sp = lax.axis_index("space")
    z, y = me // 8, lax.rem(me, 8)
    up, down = lax.rem(sp + 7, 8), lax.rem(sp + 1, 8)

    pairs = [
        (frames_h, frames_v), (cot_h, cot_v), (ws_h, ws_v), (wt_h, wt_v), (gain_h, gain_v),
        (wq_h, wq_v), (wk_h, wk_v), (wv_h, wv_v), (wo_h, wo_v),
    ]
    loads = [pltpu.make_async_copy(a, b, load_sem.at[i]) for i, (a, b) in enumerate(pairs)]

    barrier = pltpu.get_barrier_semaphore()
    for other in (up, down):
        pl.semaphore_signal(barrier, inc=1, device_id=(me, other), device_id_type=MESH)

    @pl.when(z > 0)
    def _():
        pl.semaphore_signal(barrier, inc=1, device_id=(me - 8, sp), device_id_type=MESH)

    for j in range(1, 8):
        p = z * 8 + lax.rem(y + j, 8)
        pl.semaphore_signal(barrier, inc=1, device_id=(p, sp), device_id_type=MESH)

    @pl.when(z < 7)
    def _():
        pl.semaphore_signal(barrier, inc=1, device_id=(me + 8, sp), device_id_type=MESH)

    @pl.when(jnp.logical_and(y == 0, z > 0))
    def _():
        pl.semaphore_signal(barrier, inc=1, device_id=(me - 1, sp), device_id_type=MESH)

    for copy in loads:
        copy.start()

    def halo_copies(src, dst, k):
        return [
            pltpu.make_async_remote_copy(
                src.at[:, row], dst.at[side], hs_sem.at[k + side], hr_sem.at[k + side],
                device_id=(me, other), device_id_type=MESH,
            )
            for side, (row, other) in enumerate(((3, down), (0, up)))
        ]

    def send_row(src, dst, k, row, others=8):
        for j in range(8 - others, 8):
            p = row * 8 + lax.rem(y + j, 8)
            pltpu.make_async_remote_copy(
                src.at[p], dst.at[me], s_sem.at[k], r_sem.at[k],
                device_id=(p, sp), device_id_type=MESH,
            ).start()

    def send_before(src, dst, k):
        send_row(src, dst, k, z, 7)

        def go(i, carry):
            send_row(src, dst, k, z - i)
            return carry

        lax.fori_loop(1, z + 1, go, 0)
        dst[me] = src[me]

    def send_all(src, dst, k):
        def go(i, carry):
            send_row(src, dst, k, lax.rem(z + i, 8))
            return carry

        lax.fori_loop(1, 8, go, 0)
        send_row(src, dst, k, z, 7)
        dst[me] = src[me]

    def send_ascending(src, dst, k):
        def go(i, carry):
            send_row(src, dst, k, i)
            return carry

        lax.fori_loop(0, z, go, 0)
        send_row(src, dst, k, z, 7)
        lax.fori_loop(z + 1, 8, go, 0)
        dst[me] = src[me]

    def wait_all(dst, sem):
        pltpu.make_async_copy(dst.at[pl.ds(0, 63)], dst.at[pl.ds(0, 63)], sem).wait()

    row_m, col_n = iota((T, T), 0), iota((T, T), 1)

    def natural(token):
        return token // 4 % 2 * 256 + token // 8 * 4 + token % 4

    def of_pixel(token):
        return token % 128 * 4 + token // 128

    def one_hot(wanted, other):
        return (wanted == other).astype(F32).astype(BF)

    to_msg_v[...] = one_hot(natural(row_m), col_n)

    def taps(src, weight, pick):
        for col_tap, acc in enumerate((acc0, acc1, acc2)):
            for f in range(2):
                x = src[f].reshape(256, C)
                acc[f] = pick(x, weight, 1, col_tap)
                acc[f, 64:256] += pick(x[0:192], weight, 0, col_tap)
                acc[f, 0:192] += pick(x[64:256], weight, 2, col_tap)

    def edges(halo, weight, pick):
        keep_up = jnp.where(sp > 0, 1.0, 0.0)
        keep_down = jnp.where(sp < 7, 1.0, 0.0)
        above = halo[0].reshape(128, C)
        below = halo[1].reshape(128, C)
        for col_tap, acc in enumerate((acc0, acc1, acc2)):
            first = pick(above, weight, 0, col_tap) * keep_up
            last = pick(below, weight, 2, col_tap) * keep_down
            for f in range(2):
                acc[f, 0:64] += first[f * 64 : f * 64 + 64]
                acc[f, 192:256] += last[f * 64 : f * 64 + 64]

    def columns(f, low, high):
        rows = slice(low * 64, high * 64)
        col = iota(((high - low) * 64, C), 0) % 64
        before = jnp.where(col == 0, 0.0, roll_rows(acc0[f, rows], 1))
        after = jnp.where(col == 63, 0.0, roll_rows(acc2[f, rows], -1))
        return before + acc1[f, rows] + after

    def pick_forward(x, weight, row_tap, col_tap):
        return mm(x, weight[row_tap, col_tap])

    def pick_backward(x, weight, row_tap, col_tap):
        return mm_nt(x, weight[2 - row_tap, 2 - col_tap])

    met = 9 + jnp.where(z > 0, 1, 0) + jnp.where(z < 7, 1, 0)
    met += jnp.where(jnp.logical_and(y == 7, z < 7), 1, 0)
    pl.semaphore_wait(barrier, met)
    halos = halo_copies(frames_h, halo_v, 0)
    for copy in halos:
        copy.start()

    def frame_copy(part, rows):
        return pltpu.make_async_remote_copy(
            spat_v.at[:, rows], prev_v.at[:, rows], fs_sem.at[part], fr_sem.at[part],
            device_id=(me + 1, sp), device_id_type=MESH,
        )

    shifts = [frame_copy(0, pl.ds(1, 2)), frame_copy(1, pl.ds(0, 1)), frame_copy(2, pl.ds(3, 1))]

    def spatial_rows(low, high):
        for f in range(2):
            rows = columns(f, low, high).astype(BF)
            spat_v[f, low:high] = rows.reshape(high - low, 64, C)

    loads[0].wait()
    loads[2].wait()
    taps(frames_v, ws_v, pick_forward)
    spatial_rows(1, 3)

    @pl.when(me < 63)
    def _():
        shifts[0].start()

    @pl.when(z > 0)
    def _():
        pl.semaphore_wait(before_sem, 1)

    @pl.when(z < 7)
    def _():
        pl.semaphore_signal(before_sem, inc=1, device_id=(me + 8, sp), device_id_type=MESH)

    def tell(i, carry):
        pl.semaphore_signal(
            row_sem.at[z], inc=1, device_id=((z - i) * 8 + y, sp), device_id_type=MESH
        )
        return carry

    lax.fori_loop(1, z + 1, tell, 0)

    for copy in halos:
        copy.wait()
    edges(halo_v, ws_v, pick_forward)
    spatial_rows(0, 1)
    spatial_rows(3, 4)

    @pl.when(me < 63)
    def _():
        shifts[1].start()
        shifts[2].start()

    loads[1].wait()
    ct_s[...] = to_tiles(mm(to_msg_v[...], cot_v[...].reshape(T, C)))
    send_before(ct_s, ct_r, 0)
    for copy in loads[3:]:
        copy.wait()
    now = [spat_v[f].reshape(256, C) for f in range(2)]
    acc0[0] = frames_v[0].reshape(256, C).astype(F32) + mm(now[0], wt_v[0])
    acc0[1] = frames_v[1].reshape(256, C).astype(F32) + mm(now[1], wt_v[0]) + mm(now[0], wt_v[1])
    def later_cot(row, carry):
        pl.semaphore_wait(row_sem.at[row], 1)
        send_row(ct_s, ct_r, 0, row)
        return carry

    lax.fori_loop(z + 1, 8, later_cot, 0)

    @pl.when(me > 0)
    def _():
        for copy in shifts:
            copy.wait_recv()

    @pl.when(me == 0)
    def _():
        prev_v[...] = jnp.zeros_like(prev_v)

    past = [prev_v[f].reshape(256, C) for f in range(2)]
    acc0[0] += mm(past[1], wt_v[1]) + mm(past[0], wt_v[2])
    acc0[1] += mm(past[1], wt_v[2])
    hd_s[...] = to_tiles(mm(to_msg_v[...], acc0[...].reshape(T, C).astype(BF)))
    send_before(hd_s, hd_r, 1)

    def later(row, carry):
        send_row(hd_s, hd_r, 1, row)
        return carry

    lax.fori_loop(z + 1, 8, later, 0)

    from_msg_v[...] = one_hot(natural(col_n), row_m)
    by_pixel_v[...] = one_hot(of_pixel(row_m), col_n)
    by_frame_v[...] = one_hot(of_pixel(col_n), row_m)
    wait_all(ct_r, r_sem.at[0])
    cot_n = from_tiles(ct_r[...]).astype(BF)
    cot_p = mm(by_pixel_v[...], cot_n).astype(BF)
    out_grad = mm_nt(cot_p, wo_v[...]).astype(BF)
    wait_all(hd_r, r_sem.at[1])
    token = iota((T, C), 0)
    hidden = mm(by_pixel_v[...], from_tiles(hd_r[...]).astype(BF))
    gain = gain_v[...]
    inverse = lax.rsqrt(jnp.mean(hidden * hidden, axis=-1, keepdims=True) + EPSILON)
    normed = (hidden * inverse * gain).astype(BF)
    query = mm(normed, wq_v[...]).astype(BF)
    key = mm(normed, wk_v[...]).astype(BF)
    value = mm(normed, wv_v[...]).astype(BF)
    scale = 1.0 / 16.0
    causal = iota((128, 128), 1) <= iota((128, 128), 0)
    parts = [slice(p * 128, p * 128 + 128) for p in range(4)]
    scores = [mm_nt(query[r], key[r]) for r in parts]
    prob_grad = [mm_nt(out_grad[r], value[r]) for r in parts]
    weights = [jnp.where(causal, jnp.exp(x * scale), 0.0) for x in scores]
    probs = [w / jnp.sum(w, axis=-1, keepdims=True) for w in weights]
    centre = [jnp.sum(p * g, axis=-1, keepdims=True) for p, g in zip(probs, prob_grad)]
    score_grad = [
        (p * (g - c) * scale).astype(BF) for p, g, c in zip(probs, prob_grad, centre)
    ]
    dv = [mm_tn(p.astype(BF), out_grad[r]).astype(BF) for p, r in zip(probs, parts)]
    dq = [mm(g, key[r]).astype(BF) for g, r in zip(score_grad, parts)]
    dk = [mm_tn(g, query[r]).astype(BF) for g, r in zip(score_grad, parts)]
    normed_grad = (
        mm_nt(jnp.concatenate(dq, 0), wq_v[...])
        + mm_nt(jnp.concatenate(dk, 0), wk_v[...])
        + mm_nt(jnp.concatenate(dv, 0), wv_v[...])
    )
    scaled = normed_grad * gain
    mean = jnp.mean(hidden * scaled, axis=-1, keepdims=True)
    attn_grad = (inverse * scaled - hidden * (inverse * inverse * inverse) * mean).astype(BF)
    total_p = (cot_p.astype(F32) + attn_grad.astype(F32)).astype(BF)
    total_f = mm(by_frame_v[...], total_p)
    total_n = total_f.astype(BF)
    sgrad = (
        mm_nt(total_n, wt_v[0])
        + jnp.where(token >= T - 4, 0.0, roll_rows(mm_nt(total_n, wt_v[1]), -4))
        + jnp.where(token >= T - 8, 0.0, roll_rows(mm_nt(total_n, wt_v[2]), -8))
    )
    sg_s[...] = to_tiles(sgrad)
    send_ascending(sg_s, sg_r, 2)
    tg_s[...] = to_tiles(total_f)
    wait_all(sg_s, s_sem.at[2])
    send_ascending(tg_s, tg_r, 3)

    wait_all(sg_r, r_sem.at[2])
    gnat_v[...] = mm(from_msg_v[...], from_tiles(sg_r[...]).astype(BF)).astype(BF).reshape(2, 4, 64, C)
    ghalos = halo_copies(gnat_v, ghalo_v, 2)
    for copy in ghalos:
        copy.start()
    taps(gnat_v, ws_v, pick_backward)
    for copy in ghalos:
        copy.wait()
    edges(ghalo_v, ws_v, pick_backward)
    wait_all(tg_r, r_sem.at[3])
    total = mm(from_msg_v[...], from_tiles(tg_r[...]).astype(BF))
    for f in range(2):
        out_v[f] = (total[f * 256 : f * 256 + 256] + columns(f, 0, 4)).astype(BF).reshape(4, 64, C)

    @pl.when(me < 63)
    def _():
        for copy in shifts:
            copy.wait_send()

    for k, src in ((0, ct_s), (1, hd_s), (3, tg_s)):
        wait_all(src, s_sem.at[k])


def body(frames, cotangent, w_spatial, w_temporal, norm_gain, w_query, w_key, w_value, w_out):
    big = (2, 4, 64, C)
    square = (C, C)
    vmem = pltpu.VMEM
    dma = pltpu.SemaphoreType.DMA
    message = vmem((64, 16, 128), BF)
    arrays = (frames, cotangent, w_spatial, w_temporal, norm_gain.reshape(1, C), w_query, w_key, w_value, w_out)
    arrays = [pltpu.with_memory_space_constraint(a, pltpu.HBM) for a in arrays]
    return pl.pallas_call(
        kernel,
        out_shape=jax.ShapeDtypeStruct(big, BF),
        in_specs=[pl.BlockSpec(memory_space=pl.ANY)] * 9,
        out_specs=pl.BlockSpec(memory_space=pltpu.VMEM),
        scratch_shapes=[
            vmem(big, BF), vmem(big, BF), vmem((3, 3, C, C), BF), vmem((3, C, C), BF), vmem((1, C), F32),
            vmem(square, BF), vmem(square, BF), vmem(square, BF), vmem(square, BF),
            vmem((2, 2, 64, C), BF), vmem((2, 2, 64, C), BF), vmem(big, BF), vmem(big, BF), vmem(big, BF),
            vmem((2, 256, C), F32), vmem((2, 256, C), F32), vmem((2, 256, C), F32),
            message, message, message, message, message, message, message, message,
            vmem((T, T), BF), vmem((T, T), BF), vmem((T, T), BF), vmem((T, T), BF),
            dma((9,)), dma((4,)), dma((4,)), dma((4,)), dma((4,)), dma((3,)), dma((3,)),
            pltpu.SemaphoreType.REGULAR, pltpu.SemaphoreType.REGULAR((8,)),
        ],
        compiler_params=pltpu.CompilerParams(
            collective_id=0, has_side_effects=True, vmem_limit_bytes=48 * 1024 * 1024
        ),
        name="whole",
    )(*arrays)


def solution(mesh):
    return jax.shard_map(
        body,
        mesh=mesh,
        in_specs=(
            P("tm", "space", None, None),
            P("tm", "space", None, None),
            P(),
            P(),
            P(),
            P(),
            P(),
            P(),
            P(),
        ),
        out_specs=P("tm", "space", None, None),
        check_vma=False,
    )
```

```python
import jax
import jax.numpy as jnp
from jax import lax
from jax.experimental import pallas as pl
from jax.experimental.pallas import tpu as pltpu
from jax.sharding import PartitionSpec as P

EPSILON = 1e-05
MESH = pl.DeviceIdType.MESH
BF = jnp.bfloat16
F32 = jnp.float32
T = 512
C = 256


def mm(a, b):
    return jnp.dot(a, b, preferred_element_type=F32)


def mm_nt(a, b):
    return lax.dot_general(a, b, (((1,), (1,)), ((), ())), preferred_element_type=F32)


def mm_tn(a, b):
    return lax.dot_general(a, b, (((0,), (0,)), ((), ())), preferred_element_type=F32)


def iota(shape, dim):
    return lax.broadcasted_iota(jnp.int32, shape, dim)


def to_tiles(x):
    x = x.reshape(64, 8, C)
    return jnp.concatenate([x[:, :, :128], x[:, :, 128:]], axis=1).astype(BF)


def from_tiles(x):
    x = x.astype(F32)
    return jnp.concatenate([x[:, :8], x[:, 8:]], axis=2).reshape(-1, C)


def roll_rows(x, distance):
    return pltpu.roll(x, distance % x.shape[0], 0)


def kernel(
    frames_h, cot_h, ws_h, wt_h, gain_h, wq_h, wk_h, wv_h, wo_h, out_v,
    frames_v, cot_v, ws_v, wt_v, gain_v, wq_v, wk_v, wv_v, wo_v,
    halo_v, ghalo_v, gnat_v, spat_v, prev_v, acc0, acc1, acc2,
    ct_s, hd_s, sg_s, tg_s, ct_r, hd_r, sg_r, tg_r, to_msg_v, from_msg_v, by_pixel_v, by_frame_v,
    load_sem, hs_sem, hr_sem, s_sem, r_sem, fs_sem, fr_sem, before_sem, row_sem,
):
    me = lax.axis_index("tm")
    sp = lax.axis_index("space")
    z, y = me // 8, lax.rem(me, 8)
    up, down = lax.rem(sp + 7, 8), lax.rem(sp + 1, 8)

    pairs = [
        (frames_h, frames_v), (cot_h, cot_v), (ws_h, ws_v), (wt_h, wt_v), (gain_h, gain_v),
        (wq_h, wq_v), (wk_h, wk_v), (wv_h, wv_v), (wo_h, wo_v),
    ]
    loads = [pltpu.make_async_copy(a, b, load_sem.at[i]) for i, (a, b) in enumerate(pairs)]

    barrier = pltpu.get_barrier_semaphore()
    for other in (up, down):
        pl.semaphore_signal(barrier, inc=1, device_id=(me, other), device_id_type=MESH)

    @pl.when(z > 0)
    def _():
        pl.semaphore_signal(barrier, inc=1, device_id=(me - 8, sp), device_id_type=MESH)

    for j in range(1, 8):
        p = z * 8 + lax.rem(y + j, 8)
        pl.semaphore_signal(barrier, inc=1, device_id=(p, sp), device_id_type=MESH)

    @pl.when(z < 7)
    def _():
        pl.semaphore_signal(barrier, inc=1, device_id=(me + 8, sp), device_id_type=MESH)

    @pl.when(jnp.logical_and(y == 0, z > 0))
    def _():
        pl.semaphore_signal(barrier, inc=1, device_id=(me - 1, sp), device_id_type=MESH)

    for copy in loads:
        copy.start()

    def halo_copies(src, dst, k):
        return [
            pltpu.make_async_remote_copy(
                src.at[:, row], dst.at[side], hs_sem.at[k + side], hr_sem.at[k + side],
                device_id=(me, other), device_id_type=MESH,
            )
            for side, (row, other) in enumerate(((3, down), (0, up)))
        ]

    def send_row(src, dst, k, row, others=8, r=None):
        for j in range(8 - others, 8):
            p = row * 8 + lax.rem(y + j, 8)
            pltpu.make_async_remote_copy(
                src.at[p], dst.at[me], s_sem.at[k], r_sem.at[k if r is None else r],
                device_id=(p, sp), device_id_type=MESH,
            ).start()

    def send_before(src, dst, k, r=None):
        send_row(src, dst, k, z, 7, r)

        def go(i, carry):
            send_row(src, dst, k, z - i, 8, r)
            return carry

        lax.fori_loop(1, z + 1, go, 0)
        dst[me] = src[me]

    def send_all(src, dst, k):
        def go(i, carry):
            send_row(src, dst, k, lax.rem(z + i, 8))
            return carry

        lax.fori_loop(1, 8, go, 0)
        send_row(src, dst, k, z, 7)
        dst[me] = src[me]

    def send_ascending(src, dst, k):
        def go(i, carry):
            send_row(src, dst, k, i)
            return carry

        lax.fori_loop(0, z, go, 0)
        send_row(src, dst, k, z, 7)
        lax.fori_loop(z + 1, 8, go, 0)
        dst[me] = src[me]

    def wait_all(dst, sem):
        pltpu.make_async_copy(dst.at[pl.ds(0, 63)], dst.at[pl.ds(0, 63)], sem).wait()

    row_m, col_n = iota((T, T), 0), iota((T, T), 1)

    def natural(token):
        return token // 4 % 2 * 256 + token // 8 * 4 + token % 4

    def of_pixel(token):
        return token % 64 * 4 + token // 64

    def one_hot(wanted, other):
        return (wanted == other).astype(F32).astype(BF)

    to_msg_v[...] = one_hot(natural(row_m), col_n)

    def taps(src, weight, pick):
        for col_tap, acc in enumerate((acc0, acc1, acc2)):
            for f in range(2):
                x = src[f].reshape(256, C)
                acc[f] = pick(x, weight, 1, col_tap)
                acc[f, 64:256] += pick(x[0:192], weight, 0, col_tap)
                acc[f, 0:192] += pick(x[64:256], weight, 2, col_tap)

    def edges(halo, weight, pick):
        keep_up = jnp.where(sp > 0, 1.0, 0.0)
        keep_down = jnp.where(sp < 7, 1.0, 0.0)
        above = halo[0].reshape(128, C)
        below = halo[1].reshape(128, C)
        for col_tap, acc in enumerate((acc0, acc1, acc2)):
            first = pick(above, weight, 0, col_tap) * keep_up
            last = pick(below, weight, 2, col_tap) * keep_down
            for f in range(2):
                acc[f, 0:64] += first[f * 64 : f * 64 + 64]
                acc[f, 192:256] += last[f * 64 : f * 64 + 64]

    def columns(f, low, high):
        rows = slice(low * 64, high * 64)
        col = iota(((high - low) * 64, C), 0) % 64
        before = jnp.where(col == 0, 0.0, roll_rows(acc0[f, rows], 1))
        after = jnp.where(col == 63, 0.0, roll_rows(acc2[f, rows], -1))
        return before + acc1[f, rows] + after

    def pick_forward(x, weight, row_tap, col_tap):
        return mm(x, weight[row_tap, col_tap])

    def pick_backward(x, weight, row_tap, col_tap):
        return mm_nt(x, weight[2 - row_tap, 2 - col_tap])

    met = 9 + jnp.where(z > 0, 1, 0) + jnp.where(z < 7, 1, 0)
    met += jnp.where(jnp.logical_and(y == 7, z < 7), 1, 0)
    pl.semaphore_wait(barrier, met)
    halos = halo_copies(frames_h, halo_v, 0)
    for copy in halos:
        copy.start()

    def frame_copy(part, rows):
        return pltpu.make_async_remote_copy(
            spat_v.at[:, rows], prev_v.at[:, rows], fs_sem.at[part], fr_sem.at[part],
            device_id=(me + 1, sp), device_id_type=MESH,
        )

    shifts = [frame_copy(0, pl.ds(1, 2)), frame_copy(1, pl.ds(0, 1)), frame_copy(2, pl.ds(3, 1))]

    def spatial_rows(low, high):
        for f in range(2):
            rows = columns(f, low, high).astype(BF)
            spat_v[f, low:high] = rows.reshape(high - low, 64, C)

    loads[0].wait()
    loads[2].wait()
    taps(frames_v, ws_v, pick_forward)
    spatial_rows(1, 3)

    @pl.when(me < 63)
    def _():
        shifts[0].start()

    @pl.when(z > 0)
    def _():
        pl.semaphore_wait(before_sem, 1)

    @pl.when(z < 7)
    def _():
        pl.semaphore_signal(before_sem, inc=1, device_id=(me + 8, sp), device_id_type=MESH)

    def tell(i, carry):
        pl.semaphore_signal(
            row_sem.at[z], inc=1, device_id=((z - i) * 8 + y, sp), device_id_type=MESH
        )
        return carry

    lax.fori_loop(1, z + 1, tell, 0)

    for copy in halos:
        copy.wait()
    edges(halo_v, ws_v, pick_forward)
    spatial_rows(0, 1)
    spatial_rows(3, 4)

    @pl.when(me < 63)
    def _():
        shifts[1].start()
        shifts[2].start()

    loads[1].wait()
    ct_s[...] = to_tiles(mm(to_msg_v[...], cot_v[...].reshape(T, C)))
    send_before(ct_s, ct_r, 0)
    for copy in loads[3:]:
        copy.wait()
    now = [spat_v[f].reshape(256, C) for f in range(2)]
    acc0[0] = frames_v[0].reshape(256, C).astype(F32) + mm(now[0], wt_v[0])
    acc0[1] = frames_v[1].reshape(256, C).astype(F32) + mm(now[1], wt_v[0]) + mm(now[0], wt_v[1])
    def later_cot(row, carry):
        pl.semaphore_wait(row_sem.at[row], 1)
        send_row(ct_s, ct_r, 0, row)
        return carry

    lax.fori_loop(z + 1, 8, later_cot, 0)

    @pl.when(me > 0)
    def _():
        for copy in shifts:
            copy.wait_recv()

    @pl.when(me == 0)
    def _():
        prev_v[...] = jnp.zeros_like(prev_v)

    past = [prev_v[f].reshape(256, C) for f in range(2)]
    acc0[0] += mm(past[1], wt_v[1]) + mm(past[0], wt_v[2])
    acc0[1] += mm(past[1], wt_v[2])
    hd_s[...] = to_tiles(mm(to_msg_v[...], acc0[...].reshape(T, C).astype(BF)))
    half = jnp.where(z < 4, 1, 4)
    send_before(hd_s, hd_r, 1, half)

    def later(row, carry):
        send_row(hd_s, hd_r, 1, row, 8, half)
        return carry

    lax.fori_loop(z + 1, 8, later, 0)

    from_msg_v[...] = one_hot(natural(col_n), row_m)
    row_h, col_h = iota((T // 2, T // 2), 0), iota((T // 2, T // 2), 1)
    by_pixel_v[...] = one_hot(of_pixel(row_h), col_h)
    by_frame_v[...] = one_hot(of_pixel(col_h), row_h)
    wait_all(ct_r, r_sem.at[0])
    cot_n = from_tiles(ct_r[...]).astype(BF)
    cot_p = jnp.concatenate(
        [mm(by_pixel_v[...], cot_n[:256]), mm(by_pixel_v[...], cot_n[256:])], 0
    ).astype(BF)
    out_grad = mm_nt(cot_p, wo_v[...]).astype(BF)
    gain = gain_v[...]

    def wait_half(k, mine):
        def some(count):
            part = hd_r.at[pl.ds(0, count)]
            pltpu.make_async_copy(part, part, r_sem.at[k]).wait()

        @pl.when(mine)
        def _():
            some(31)

        @pl.when(jnp.logical_not(mine))
        def _():
            some(32)

    def project_half(low):
        own = mm(by_pixel_v[...], from_tiles(hd_r[low : low + 32]).astype(BF))
        rate = lax.rsqrt(jnp.mean(own * own, axis=-1, keepdims=True) + EPSILON)
        normed = (own * rate * gain).astype(BF)
        return [own, rate] + [mm(normed, w[...]).astype(BF) for w in (wq_v, wk_v, wv_v)]

    wait_half(1, z < 4)
    first = project_half(0)
    wait_half(4, z >= 4)
    second = project_half(32)
    hidden, inverse, query, key, value = [
        jnp.concatenate([a, b], 0) for a, b in zip(first, second)
    ]
    token = iota((T, C), 0)
    scale = 1.0 / 16.0
    causal = iota((128, 128), 1) <= iota((128, 128), 0)

    def of(x, p):
        return jnp.concatenate([x[p * 64 : p * 64 + 64], x[256 + p * 64 : 320 + p * 64]], 0)

    def together(pixels):
        return jnp.concatenate([x[:64] for x in pixels] + [x[64:] for x in pixels], 0)

    queries, keys, values, grads = [
        [of(x, p) for p in range(4)] for x in (query, key, value, out_grad)
    ]
    scores = [mm_nt(q, k) for q, k in zip(queries, keys)]
    prob_grad = [mm_nt(g, v) for g, v in zip(grads, values)]
    weights = [jnp.where(causal, jnp.exp(x * scale), 0.0) for x in scores]
    probs = [w / jnp.sum(w, axis=-1, keepdims=True) for w in weights]
    centre = [jnp.sum(p * g, axis=-1, keepdims=True) for p, g in zip(probs, prob_grad)]
    score_grad = [
        (p * (g - c) * scale).astype(BF) for p, g, c in zip(probs, prob_grad, centre)
    ]
    dv = together([mm_tn(p.astype(BF), g).astype(BF) for p, g in zip(probs, grads)])
    dq = together([mm(s, k).astype(BF) for s, k in zip(score_grad, keys)])
    dk = together([mm_tn(s, q).astype(BF) for s, q in zip(score_grad, queries)])
    normed_grad = (
        mm_nt(dq, wq_v[...])
        + mm_nt(dk, wk_v[...])
        + mm_nt(dv, wv_v[...])
    )
    scaled = normed_grad * gain
    mean = jnp.mean(hidden * scaled, axis=-1, keepdims=True)
    attn_grad = (inverse * scaled - hidden * (inverse * inverse * inverse) * mean).astype(BF)
    total_p = (cot_p.astype(F32) + attn_grad.astype(F32)).astype(BF)
    total_f = jnp.concatenate(
        [mm(by_frame_v[...], total_p[:256]), mm(by_frame_v[...], total_p[256:])], 0
    )
    total_n = total_f.astype(BF)
    sgrad = (
        mm_nt(total_n, wt_v[0])
        + jnp.where(token >= T - 4, 0.0, roll_rows(mm_nt(total_n, wt_v[1]), -4))
        + jnp.where(token >= T - 8, 0.0, roll_rows(mm_nt(total_n, wt_v[2]), -8))
    )
    sg_s[...] = to_tiles(sgrad)
    send_ascending(sg_s, sg_r, 2)
    tg_s[...] = to_tiles(total_f)
    wait_all(sg_s, s_sem.at[2])
    send_ascending(tg_s, tg_r, 3)

    wait_all(sg_r, r_sem.at[2])
    gnat_v[...] = mm(from_msg_v[...], from_tiles(sg_r[...]).astype(BF)).astype(BF).reshape(2, 4, 64, C)
    ghalos = halo_copies(gnat_v, ghalo_v, 2)
    for copy in ghalos:
        copy.start()
    taps(gnat_v, ws_v, pick_backward)
    for copy in ghalos:
        copy.wait()
    edges(ghalo_v, ws_v, pick_backward)
    for f in range(2):
        acc1[f] = columns(f, 0, 4)
    wait_all(tg_r, r_sem.at[3])
    total = mm(from_msg_v[...], from_tiles(tg_r[...]).astype(BF))
    for f in range(2):
        out_v[f] = (total[f * 256 : f * 256 + 256] + acc1[f]).astype(BF).reshape(4, 64, C)

    @pl.when(me < 63)
    def _():
        for copy in shifts:
            copy.wait_send()

    for k, src in ((0, ct_s), (1, hd_s), (3, tg_s)):
        wait_all(src, s_sem.at[k])


def body(frames, cotangent, w_spatial, w_temporal, norm_gain, w_query, w_key, w_value, w_out):
    big = (2, 4, 64, C)
    square = (C, C)
    vmem = pltpu.VMEM
    dma = pltpu.SemaphoreType.DMA
    message = vmem((64, 16, 128), BF)
    arrays = (frames, cotangent, w_spatial, w_temporal, norm_gain.reshape(1, C), w_query, w_key, w_value, w_out)
    arrays = [pltpu.with_memory_space_constraint(a, pltpu.HBM) for a in arrays]
    return pl.pallas_call(
        kernel,
        out_shape=jax.ShapeDtypeStruct(big, BF),
        in_specs=[pl.BlockSpec(memory_space=pl.ANY)] * 9,
        out_specs=pl.BlockSpec(memory_space=pltpu.VMEM),
        scratch_shapes=[
            vmem(big, BF), vmem(big, BF), vmem((3, 3, C, C), BF), vmem((3, C, C), BF), vmem((1, C), F32),
            vmem(square, BF), vmem(square, BF), vmem(square, BF), vmem(square, BF),
            vmem((2, 2, 64, C), BF), vmem((2, 2, 64, C), BF), vmem(big, BF), vmem(big, BF), vmem(big, BF),
            vmem((2, 256, C), F32), vmem((2, 256, C), F32), vmem((2, 256, C), F32),
            message, message, message, message, message, message, message, message,
            vmem((T, T), BF), vmem((T, T), BF), vmem((T // 2, T // 2), BF), vmem((T // 2, T // 2), BF),
            dma((9,)), dma((4,)), dma((4,)), dma((4,)), dma((5,)), dma((3,)), dma((3,)),
            pltpu.SemaphoreType.REGULAR, pltpu.SemaphoreType.REGULAR((8,)),
        ],
        compiler_params=pltpu.CompilerParams(
            collective_id=0, has_side_effects=True, vmem_limit_bytes=48 * 1024 * 1024
        ),
        name="whole",
    )(*arrays)


def solution(mesh):
    return jax.shard_map(
        body,
        mesh=mesh,
        in_specs=(
            P("tm", "space", None, None),
            P("tm", "space", None, None),
            P(),
            P(),
            P(),
            P(),
            P(),
            P(),
            P(),
        ),
        out_specs=P("tm", "space", None, None),
        check_vma=False,
    )
```

```python
import jax
import jax.numpy as jnp
from jax import lax
from jax.experimental import pallas as pl
from jax.experimental.pallas import tpu as pltpu
from jax.sharding import PartitionSpec as P

EPSILON = 1e-05
MESH = pl.DeviceIdType.MESH
BF = jnp.bfloat16
F32 = jnp.float32
T = 512
C = 256


def mm(a, b):
    return jnp.dot(a, b, preferred_element_type=F32)


def mm_nt(a, b):
    return lax.dot_general(a, b, (((1,), (1,)), ((), ())), preferred_element_type=F32)


def mm_tn(a, b):
    return lax.dot_general(a, b, (((0,), (0,)), ((), ())), preferred_element_type=F32)


def iota(shape, dim):
    return lax.broadcasted_iota(jnp.int32, shape, dim)


def to_tiles(x):
    x = x.reshape(-1, 8, C)
    return jnp.concatenate([x[:, :, :128], x[:, :, 128:]], axis=1).astype(BF)


def from_tiles(x):
    x = x.astype(F32)
    return jnp.concatenate([x[:, :8], x[:, 8:]], axis=2).reshape(-1, C)


def roll_rows(x, distance):
    return pltpu.roll(x, distance % x.shape[0], 0)


def kernel(
    frames_h, cot_h, ws_h, wt_h, gain_h, wq_h, wk_h, wv_h, wo_h, out_v,
    frames_v, cot_v, ws_v, wt_v, gain_v, wq_v, wk_v, wv_v, wo_v,
    halo_v, ghalo_v, gnat_v, spat_v, prev_v, acc0, acc1, acc2,
    ct_s, hd_s, sg_s, tg_s, ct_r, hd_r, sg_r, tg_r, to_msg_v, from_msg_v, by_pixel_v, by_frame_v,
    load_sem, hs_sem, hr_sem, s_sem, r_sem, fs_sem, fr_sem, before_sem, row_sem,
):
    me = lax.axis_index("tm")
    sp = lax.axis_index("space")
    z, y = me // 8, lax.rem(me, 8)
    up, down = lax.rem(sp + 7, 8), lax.rem(sp + 1, 8)

    pairs = [
        (frames_h, frames_v), (cot_h, cot_v), (ws_h, ws_v), (wt_h, wt_v), (gain_h, gain_v),
        (wq_h, wq_v), (wk_h, wk_v), (wv_h, wv_v), (wo_h, wo_v),
    ]
    loads = [pltpu.make_async_copy(a, b, load_sem.at[i]) for i, (a, b) in enumerate(pairs)]

    barrier = pltpu.get_barrier_semaphore()
    for other in (up, down):
        pl.semaphore_signal(barrier, inc=1, device_id=(me, other), device_id_type=MESH)

    @pl.when(z > 0)
    def _():
        pl.semaphore_signal(barrier, inc=1, device_id=(me - 8, sp), device_id_type=MESH)

    for j in range(1, 8):
        p = z * 8 + lax.rem(y + j, 8)
        pl.semaphore_signal(barrier, inc=1, device_id=(p, sp), device_id_type=MESH)

    @pl.when(z < 7)
    def _():
        pl.semaphore_signal(barrier, inc=1, device_id=(me + 8, sp), device_id_type=MESH)

    @pl.when(jnp.logical_and(y == 0, z > 0))
    def _():
        pl.semaphore_signal(barrier, inc=1, device_id=(me - 1, sp), device_id_type=MESH)

    for copy in loads:
        copy.start()

    def halo_copies(src, dst, k):
        return [
            pltpu.make_async_remote_copy(
                src.at[:, row], dst.at[side], hs_sem.at[k + side], hr_sem.at[k + side],
                device_id=(me, other), device_id_type=MESH,
            )
            for side, (row, other) in enumerate(((3, down), (0, up)))
        ]

    def send_row(src, dst, k, row, others=8, r=None):
        for j in range(8 - others, 8):
            p = row * 8 + lax.rem(y + j, 8)
            pltpu.make_async_remote_copy(
                src.at[p], dst.at[me], s_sem.at[k], r_sem.at[k if r is None else r],
                device_id=(p, sp), device_id_type=MESH,
            ).start()

    def send_before(src, dst, k, r=None):
        send_row(src, dst, k, z, 7, r)

        def go(i, carry):
            send_row(src, dst, k, z - i, 8, r)
            return carry

        lax.fori_loop(1, z + 1, go, 0)
        dst[me] = src[me]

    def send_all(src, dst, k):
        def go(i, carry):
            send_row(src, dst, k, lax.rem(z + i, 8))
            return carry

        lax.fori_loop(1, 8, go, 0)
        send_row(src, dst, k, z, 7)
        dst[me] = src[me]

    def send_rows(src, dst, k, low, high):
        def go(row, carry):
            @pl.when(row == z)
            def _():
                send_row(src, dst, k, z, 7)

            @pl.when(row != z)
            def _():
                send_row(src, dst, k, row)

            return carry

        lax.fori_loop(low, high, go, 0)

    def wait_all(dst, sem):
        pltpu.make_async_copy(dst.at[pl.ds(0, 63)], dst.at[pl.ds(0, 63)], sem).wait()

    row_m, col_n = iota((T, T), 0), iota((T, T), 1)

    def natural(token):
        return token // 4 % 2 * 256 + token // 8 * 4 + token % 4

    def of_pixel(token):
        return token % 64 * 4 + token // 64

    def one_hot(wanted, other):
        return (wanted == other).astype(F32).astype(BF)

    to_msg_v[...] = one_hot(natural(row_m), col_n)

    def taps(src, weight, pick):
        for col_tap, acc in enumerate((acc0, acc1, acc2)):
            for f in range(2):
                x = src[f].reshape(256, C)
                acc[f] = pick(x, weight, 1, col_tap)
                acc[f, 64:256] += pick(x[0:192], weight, 0, col_tap)
                acc[f, 0:192] += pick(x[64:256], weight, 2, col_tap)

    def edges(halo, weight, pick):
        keep_up = jnp.where(sp > 0, 1.0, 0.0)
        keep_down = jnp.where(sp < 7, 1.0, 0.0)
        above = halo[0].reshape(128, C)
        below = halo[1].reshape(128, C)
        for col_tap, acc in enumerate((acc0, acc1, acc2)):
            first = pick(above, weight, 0, col_tap) * keep_up
            last = pick(below, weight, 2, col_tap) * keep_down
            for f in range(2):
                acc[f, 0:64] += first[f * 64 : f * 64 + 64]
                acc[f, 192:256] += last[f * 64 : f * 64 + 64]

    def columns(f, low, high):
        rows = slice(low * 64, high * 64)
        col = iota(((high - low) * 64, C), 0) % 64
        before = jnp.where(col == 0, 0.0, roll_rows(acc0[f, rows], 1))
        after = jnp.where(col == 63, 0.0, roll_rows(acc2[f, rows], -1))
        return before + acc1[f, rows] + after

    def pick_forward(x, weight, row_tap, col_tap):
        return mm(x, weight[row_tap, col_tap])

    def pick_backward(x, weight, row_tap, col_tap):
        return mm_nt(x, weight[2 - row_tap, 2 - col_tap])

    met = 9 + jnp.where(z > 0, 1, 0) + jnp.where(z < 7, 1, 0)
    met += jnp.where(jnp.logical_and(y == 7, z < 7), 1, 0)
    pl.semaphore_wait(barrier, met)
    halos = halo_copies(frames_h, halo_v, 0)
    for copy in halos:
        copy.start()

    def frame_copy(part, rows):
        return pltpu.make_async_remote_copy(
            spat_v.at[:, rows], prev_v.at[:, rows], fs_sem.at[part], fr_sem.at[part],
            device_id=(me + 1, sp), device_id_type=MESH,
        )

    shifts = [frame_copy(0, pl.ds(1, 2)), frame_copy(1, pl.ds(0, 1)), frame_copy(2, pl.ds(3, 1))]

    def spatial_rows(low, high):
        for f in range(2):
            rows = columns(f, low, high).astype(BF)
            spat_v[f, low:high] = rows.reshape(high - low, 64, C)

    loads[0].wait()
    loads[2].wait()
    taps(frames_v, ws_v, pick_forward)
    spatial_rows(1, 3)

    @pl.when(me < 63)
    def _():
        shifts[0].start()

    @pl.when(z > 0)
    def _():
        pl.semaphore_wait(before_sem, 1)

    @pl.when(z < 7)
    def _():
        pl.semaphore_signal(before_sem, inc=1, device_id=(me + 8, sp), device_id_type=MESH)

    def tell(i, carry):
        pl.semaphore_signal(
            row_sem.at[z], inc=1, device_id=((z - i) * 8 + y, sp), device_id_type=MESH
        )
        return carry

    lax.fori_loop(1, z + 1, tell, 0)

    for copy in halos:
        copy.wait()
    edges(halo_v, ws_v, pick_forward)
    spatial_rows(0, 1)
    spatial_rows(3, 4)

    @pl.when(me < 63)
    def _():
        shifts[1].start()
        shifts[2].start()

    loads[1].wait()
    ct_s[...] = to_tiles(mm(to_msg_v[...], cot_v[...].reshape(T, C)))
    send_before(ct_s, ct_r, 0)
    for copy in loads[3:]:
        copy.wait()
    now = [spat_v[f].reshape(256, C) for f in range(2)]
    acc0[0] = frames_v[0].reshape(256, C).astype(F32) + mm(now[0], wt_v[0])
    acc0[1] = frames_v[1].reshape(256, C).astype(F32) + mm(now[1], wt_v[0]) + mm(now[0], wt_v[1])
    def later_cot(row, carry):
        pl.semaphore_wait(row_sem.at[row], 1)
        send_row(ct_s, ct_r, 0, row)
        return carry

    lax.fori_loop(z + 1, 8, later_cot, 0)

    @pl.when(me > 0)
    def _():
        for copy in shifts:
            copy.wait_recv()

    @pl.when(me == 0)
    def _():
        prev_v[...] = jnp.zeros_like(prev_v)

    past = [prev_v[f].reshape(256, C) for f in range(2)]
    acc0[0] += mm(past[1], wt_v[1]) + mm(past[0], wt_v[2])
    acc0[1] += mm(past[1], wt_v[2])
    hd_s[...] = to_tiles(mm(to_msg_v[...], acc0[...].reshape(T, C).astype(BF)))
    half = jnp.where(z < 4, 1, 4)
    send_before(hd_s, hd_r, 1, half)

    def later(row, carry):
        send_row(hd_s, hd_r, 1, row, 8, half)
        return carry

    lax.fori_loop(z + 1, 8, later, 0)

    from_msg_v[...] = one_hot(natural(col_n), row_m)
    row_h, col_h = iota((T // 2, T // 2), 0), iota((T // 2, T // 2), 1)
    by_pixel_v[...] = one_hot(of_pixel(row_h), col_h)
    by_frame_v[...] = one_hot(of_pixel(col_h), row_h)
    wait_all(ct_r, r_sem.at[0])
    cot_n = from_tiles(ct_r[...]).astype(BF)
    cot_p = jnp.concatenate(
        [mm(by_pixel_v[...], cot_n[:256]), mm(by_pixel_v[...], cot_n[256:])], 0
    ).astype(BF)
    out_grad = mm_nt(cot_p, wo_v[...]).astype(BF)
    gain = gain_v[...]

    def wait_half(k, mine):
        def some(count):
            part = hd_r.at[pl.ds(0, count)]
            pltpu.make_async_copy(part, part, r_sem.at[k]).wait()

        @pl.when(mine)
        def _():
            some(31)

        @pl.when(jnp.logical_not(mine))
        def _():
            some(32)

    def project_half(low):
        own = mm(by_pixel_v[...], from_tiles(hd_r[low : low + 32]).astype(BF))
        rate = lax.rsqrt(jnp.mean(own * own, axis=-1, keepdims=True) + EPSILON)
        normed = (own * rate * gain).astype(BF)
        return [own, rate] + [mm(normed, w[...]).astype(BF) for w in (wq_v, wk_v, wv_v)]

    wait_half(1, z < 4)
    first = project_half(0)
    wait_half(4, z >= 4)
    second = project_half(32)
    hidden, inverse, query, key, value = [
        jnp.concatenate([a, b], 0) for a, b in zip(first, second)
    ]
    token = iota((T, C), 0)
    scale = 1.0 / 16.0
    causal = iota((128, 128), 1) <= iota((128, 128), 0)

    def of(x, p):
        return jnp.concatenate([x[p * 64 : p * 64 + 64], x[256 + p * 64 : 320 + p * 64]], 0)

    def together(pixels):
        return jnp.concatenate([x[:64] for x in pixels] + [x[64:] for x in pixels], 0)

    queries, keys, values, grads = [
        [of(x, p) for p in range(4)] for x in (query, key, value, out_grad)
    ]
    scores = [mm_nt(q, k) for q, k in zip(queries, keys)]
    prob_grad = [mm_nt(g, v) for g, v in zip(grads, values)]
    weights = [jnp.where(causal, jnp.exp(x * scale), 0.0) for x in scores]
    probs = [w / jnp.sum(w, axis=-1, keepdims=True) for w in weights]
    centre = [jnp.sum(p * g, axis=-1, keepdims=True) for p, g in zip(probs, prob_grad)]
    score_grad = [
        (p * (g - c) * scale).astype(BF) for p, g, c in zip(probs, prob_grad, centre)
    ]
    dv = together([mm_tn(p.astype(BF), g).astype(BF) for p, g in zip(probs, grads)])
    dq = together([mm(s, k).astype(BF) for s, k in zip(score_grad, keys)])
    dk = together([mm_tn(s, q).astype(BF) for s, q in zip(score_grad, queries)])
    normed_grad = (
        mm_nt(dq, wq_v[...])
        + mm_nt(dk, wk_v[...])
        + mm_nt(dv, wv_v[...])
    )
    scaled = normed_grad * gain
    mean = jnp.mean(hidden * scaled, axis=-1, keepdims=True)
    attn_grad = (inverse * scaled - hidden * (inverse * inverse * inverse) * mean).astype(BF)
    total_p = (cot_p.astype(F32) + attn_grad.astype(F32)).astype(BF)
    total_f = jnp.concatenate(
        [mm(by_frame_v[...], total_p[:256]), mm(by_frame_v[...], total_p[256:])], 0
    )
    total_n = total_f.astype(BF)
    ahead = total_n[:272]
    sg_s[0:32] = to_tiles(
        mm_nt(total_n[:256], wt_v[0])
        + roll_rows(mm_nt(ahead, wt_v[1]), -4)[:256]
        + mm_nt(ahead, wt_v[2])[8:264]
    )
    send_rows(sg_s, sg_r, 2, 0, 4)
    last = total_n[256:]
    token = iota((T // 2, C), 0)
    sg_s[32:64] = to_tiles(
        mm_nt(last, wt_v[0])
        + jnp.where(token >= 252, 0.0, roll_rows(mm_nt(last, wt_v[1]), -4))
        + jnp.where(token >= 248, 0.0, roll_rows(mm_nt(last, wt_v[2]), -8))
    )
    send_rows(sg_s, sg_r, 2, 4, 8)
    sg_r[me] = sg_s[me]
    tg_s[...] = to_tiles(total_f)
    wait_all(sg_s, s_sem.at[2])
    send_rows(tg_s, tg_r, 3, 0, 8)
    tg_r[me] = tg_s[me]

    wait_all(sg_r, r_sem.at[2])
    gnat_v[...] = mm(from_msg_v[...], from_tiles(sg_r[...]).astype(BF)).astype(BF).reshape(2, 4, 64, C)
    ghalos = halo_copies(gnat_v, ghalo_v, 2)
    for copy in ghalos:
        copy.start()
    taps(gnat_v, ws_v, pick_backward)
    for copy in ghalos:
        copy.wait()
    edges(ghalo_v, ws_v, pick_backward)
    for f in range(2):
        acc1[f] = columns(f, 0, 4)
    wait_all(tg_r, r_sem.at[3])
    total = mm(from_msg_v[...], from_tiles(tg_r[...]).astype(BF))
    for f in range(2):
        out_v[f] = (total[f * 256 : f * 256 + 256] + acc1[f]).astype(BF).reshape(4, 64, C)

    @pl.when(me < 63)
    def _():
        for copy in shifts:
            copy.wait_send()

    for k, src in ((0, ct_s), (1, hd_s), (3, tg_s)):
        wait_all(src, s_sem.at[k])


def body(frames, cotangent, w_spatial, w_temporal, norm_gain, w_query, w_key, w_value, w_out):
    big = (2, 4, 64, C)
    square = (C, C)
    vmem = pltpu.VMEM
    dma = pltpu.SemaphoreType.DMA
    message = vmem((64, 16, 128), BF)
    arrays = (frames, cotangent, w_spatial, w_temporal, norm_gain.reshape(1, C), w_query, w_key, w_value, w_out)
    arrays = [pltpu.with_memory_space_constraint(a, pltpu.HBM) for a in arrays]
    return pl.pallas_call(
        kernel,
        out_shape=jax.ShapeDtypeStruct(big, BF),
        in_specs=[pl.BlockSpec(memory_space=pl.ANY)] * 9,
        out_specs=pl.BlockSpec(memory_space=pltpu.VMEM),
        scratch_shapes=[
            vmem(big, BF), vmem(big, BF), vmem((3, 3, C, C), BF), vmem((3, C, C), BF), vmem((1, C), F32),
            vmem(square, BF), vmem(square, BF), vmem(square, BF), vmem(square, BF),
            vmem((2, 2, 64, C), BF), vmem((2, 2, 64, C), BF), vmem(big, BF), vmem(big, BF), vmem(big, BF),
            vmem((2, 256, C), F32), vmem((2, 256, C), F32), vmem((2, 256, C), F32),
            message, message, message, message, message, message, message, message,
            vmem((T, T), BF), vmem((T, T), BF), vmem((T // 2, T // 2), BF), vmem((T // 2, T // 2), BF),
            dma((9,)), dma((4,)), dma((4,)), dma((4,)), dma((5,)), dma((3,)), dma((3,)),
            pltpu.SemaphoreType.REGULAR, pltpu.SemaphoreType.REGULAR((8,)),
        ],
        compiler_params=pltpu.CompilerParams(
            collective_id=0, has_side_effects=True, vmem_limit_bytes=48 * 1024 * 1024
        ),
        name="whole",
    )(*arrays)


def solution(mesh):
    return jax.shard_map(
        body,
        mesh=mesh,
        in_specs=(
            P("tm", "space", None, None),
            P("tm", "space", None, None),
            P(),
            P(),
            P(),
            P(),
            P(),
            P(),
            P(),
        ),
        out_specs=P("tm", "space", None, None),
        check_vma=False,
    )
```
